32 devices in a mesh: row: 4 (over z), col: 8 (over y, x, core).
Axes of the slice: x: 2, y: 2, z: 4, core: 2. Of those that a mesh axis runs over, the one named last changes fastest.
Arguments:
- vectors: bfloat16 [16384, 256], P(('row', 'col')), may hold values from -6 to 6
- blocks: bfloat16 [4, 8, 256, 128, 128], P('row', 'col'), may hold values from -0.046875 to 0.046875
- block_rows: int32 [4, 8, 256], P('row', 'col'), may hold values from 0 to 31
- block_cols: int32 [4, 8, 256], P('row', 'col'), may hold values from 0 to 15
- block_count: int32 [4, 8], P('row', 'col'), may hold values from 32 to 256, as said below
- lower_edge: float32 [1], replicated, may hold values from -0.6 to -0.3
- upper_edge: float32 [1], replicated, may hold values from 1 to 2
Outputs:
- filtered: float32 [16384, 256], P(('row', 'col'))
The draws below stay inside these ranges and needn't reach their ends.
Inputs may be any that keep to these rules, and one draw needn't show every extreme that they name: `block_count`: some device has all 256 slots live.
All inputs are finite; a program needn't handle non-finite values.
Results may differ from the reference program's by a relative error of at most 0.008.
Values may be sent and summed in bfloat16 or wider, within the bound.
A program may use at most 192 MiB of HBM per device.

```python
import jax
import jax.numpy as jnp
from jax import lax

BLOCK = 128
VECS = 256
SEG = 512
BLK_DEV = 256
DEGREE = 2
ORDER = 16384
N_ROW = 4
N_COL = 8


def draw_block_count(key, part):
    key = jax.random.fold_in(key, 7)
    key_counts, key_busy = jax.random.split(key)
    counts = jax.random.randint(key_counts, (N_ROW, N_COL), BLK_DEV // 8, BLK_DEV // 2 + 1)
    busiest = jax.random.randint(key_busy, (), 0, N_ROW * N_COL)
    flattened = jnp.where(jnp.arange(N_ROW * N_COL) == busiest, BLK_DEV, counts.reshape(-1))
    return flattened.reshape(N_ROW, N_COL).astype(jnp.int32)


def touch_ends(entries, own_key, least, largest):
    index_at = [jax.random.randint(jax.random.fold_in(own_key, axis), (), 0, length) for axis, length in enumerate(entries.shape)]
    main_axis = entries.shape.index(max(entries.shape))
    neighbour = index_at[:main_axis] + [(index_at[main_axis] + 1) % entries.shape[main_axis]] + index_at[main_axis + 1:]
    return entries.at[tuple(index_at)].set(least).at[tuple(neighbour)].set(largest)


def level_of(own_key, dims, pieces, smallest, largest):
    def one(dim, parts):
        steps = jax.random.uniform(jax.random.fold_in(jax.random.fold_in(own_key, 6), dim), (parts,), jnp.float32, smallest / len(pieces), largest / len(pieces))
        return jnp.repeat(jnp.exp(steps), dims[dim] // parts).reshape((-1,) + (1,) * (len(dims) - dim - 1))

    loudness = one(*pieces[0])
    for cut in pieces[1:]:
        loudness = loudness * one(*cut)
    return loudness


def bell_draw(stream_key, dims, scale, reach, cuts=(), held_as=jnp.bfloat16):
    array = scale * jax.random.normal(stream_key, dims, jnp.float32)
    if cuts:
        array = array * level_of(stream_key, dims, cuts, -0.22, 0.18)
    return jnp.clip(array, -reach, reach).astype(held_as)


def setup_inputs(seed: int = 0) -> dict:
    arg_keys = jax.random.split(jax.random.key(seed), 8)
    vectors = bell_draw(arg_keys[0], (ORDER, VECS), 1.0, 6.0, ((0, 32),))
    blocks = bell_draw(arg_keys[1], (N_ROW, N_COL, BLK_DEV, BLOCK, BLOCK), (2 * BLK_DEV * BLOCK * BLOCK // SEG) ** -0.5, 0.046875, ((0, 4), (1, 8)))
    block_rows = touch_ends(jax.random.randint(arg_keys[2], (N_ROW, N_COL, BLK_DEV), 0, N_COL * SEG // BLOCK), jax.random.fold_in(arg_keys[2], 1), 0, (N_COL * SEG // BLOCK) - 1).astype(jnp.int32)
    block_cols = touch_ends(jax.random.randint(arg_keys[3], (N_ROW, N_COL, BLK_DEV), 0, N_ROW * SEG // BLOCK), jax.random.fold_in(arg_keys[3], 1), 0, (N_ROW * SEG // BLOCK) - 1).astype(jnp.int32)
    block_count = draw_block_count(jax.random.fold_in(arg_keys[7], 71), 0)
    lower_edge = jnp.clip(jax.random.uniform(arg_keys[5], (1,), jnp.float32, -0.6, -0.3), -0.6, -0.3)
    upper_edge = jnp.clip(jax.random.uniform(arg_keys[6], (1,), jnp.float32, 1.0, 2.0), 1.0, 2.0)
    return {"vectors": vectors, "blocks": blocks, "block_rows": block_rows, "block_cols": block_cols, "block_count": block_count, "lower_edge": lower_edge, "upper_edge": upper_edge}


def applied_product(operand, blocks, block_rows, block_cols, block_count):
    vec_width = operand.shape[1]
    vector_grid = operand.reshape(N_ROW, N_COL, SEG, vec_width)

    def device_step(totals, device):
        row_pos = device // N_COL
        col_pos = device % N_COL
        rows_side = lax.dynamic_index_in_dim(vector_grid, row_pos, 0, keepdims=False).reshape(-1, BLOCK, vec_width)
        cols_side = lax.dynamic_index_in_dim(vector_grid, col_pos, 1, keepdims=False).reshape(-1, BLOCK, vec_width)
        row_blocks = lax.dynamic_index_in_dim(blocks, row_pos, 0, keepdims=False)
        block_tile = lax.dynamic_index_in_dim(row_blocks, col_pos, 0, keepdims=False).astype(jnp.float32)
        rows_here = block_rows[row_pos, col_pos]
        cols_here = block_cols[row_pos, col_pos]
        live_mask = (jnp.arange(BLK_DEV) < block_count[row_pos, col_pos]).astype(jnp.float32)[:, None, None]
        forward = jnp.einsum('gij,gjv->giv', block_tile, cols_side[cols_here].astype(jnp.float32)) * live_mask
        mirror = jnp.einsum('gji,gjv->giv', block_tile, rows_side[rows_here].astype(jnp.float32)) * live_mask
        row_part = jnp.zeros(rows_side.shape, jnp.float32).at[rows_here].add(forward)
        col_part = jnp.zeros(cols_side.shape, jnp.float32).at[cols_here].add(mirror)
        totals = totals.at[row_pos].add(row_part.reshape(N_COL, SEG, vec_width))
        totals = totals.at[:, col_pos].add(col_part.reshape(N_ROW, SEG, vec_width))
        return totals, None

    totals = jnp.zeros((N_ROW, N_COL, SEG, vec_width), jnp.float32)
    totals, unused = lax.scan(device_step, totals, jnp.arange(N_ROW * N_COL, dtype=jnp.int32))
    return totals.reshape(-1, vec_width)


def reference(vectors, blocks, block_rows, block_cols, block_count, lower_edge, upper_edge):
    center = (upper_edge[0] + lower_edge[0]) * 0.5
    half_width = (upper_edge[0] - lower_edge[0]) * 0.5
    current = vectors.astype(jnp.float32)
    previous = jnp.zeros_like(current)
    for degree in range(DEGREE):
        operand = current.astype(jnp.bfloat16)
        applied = applied_product(operand, blocks, block_rows, block_cols, block_count)
        shifted = applied - center * current
        if degree == 0:
            following = shifted / half_width
        else:
            following = 2.0 * shifted / half_width - previous
        previous, current = current, following
    return current
```

```python
import functools

import jax
import jax.numpy as jnp
from jax import lax
from jax.experimental import pallas as pl
from jax.experimental.pallas import tpu as pltpu
from jax.sharding import PartitionSpec as P

MESH = pl.DeviceIdType.MESH

DEGREE = 2


def pick_table(indices, count):
    return (indices[:, None] == jnp.arange(count, dtype=jnp.int32)[None, :]).astype(jnp.bfloat16)


def place_sum(table, values):
    upper = values.astype(jnp.bfloat16)
    lower = (values - upper.astype(jnp.float32)).astype(jnp.bfloat16)
    first = jnp.einsum("gt,giv->tiv", table, upper, preferred_element_type=jnp.float32)
    second = jnp.einsum("gt,giv->tiv", table, lower, preferred_element_type=jnp.float32)
    return first + second


def slot_products(
    local_blocks, local_rows, local_cols, slot_count, rows_side, cols_side, group_size, group_limit
):
    block_size = local_blocks.shape[1]
    vec_width = rows_side.shape[1]
    row_tiles = rows_side.reshape(-1, block_size, vec_width)
    col_tiles = cols_side.reshape(-1, block_size, vec_width)
    row_count = row_tiles.shape[0]
    col_count = col_tiles.shape[0]

    def group_step(position, totals):
        row_totals, col_totals = totals
        first_slot = position * group_size
        block_tile = lax.dynamic_slice_in_dim(local_blocks, first_slot, group_size, 0)
        rows_here = lax.dynamic_slice_in_dim(local_rows, first_slot, group_size, 0)
        cols_here = lax.dynamic_slice_in_dim(local_cols, first_slot, group_size, 0)
        live_mask = (first_slot + jnp.arange(group_size) < slot_count).astype(jnp.float32)[
            :, None, None
        ]
        row_table = pick_table(rows_here, row_count)
        col_table = pick_table(cols_here, col_count)
        col_picked = jnp.einsum(
            "gt,tjv->gjv", col_table, col_tiles, preferred_element_type=jnp.float32
        ).astype(jnp.bfloat16)
        row_picked = jnp.einsum(
            "gt,tjv->gjv", row_table, row_tiles, preferred_element_type=jnp.float32
        ).astype(jnp.bfloat16)
        forward = (
            jnp.einsum("gij,gjv->giv", block_tile, col_picked, preferred_element_type=jnp.float32)
            * live_mask
        )
        mirror = (
            jnp.einsum("gji,gjv->giv", block_tile, row_picked, preferred_element_type=jnp.float32)
            * live_mask
        )
        return (
            row_totals + place_sum(row_table, forward),
            col_totals + place_sum(col_table, mirror),
        )

    start_totals = (
        jnp.zeros(row_tiles.shape, jnp.float32),
        jnp.zeros(col_tiles.shape, jnp.float32),
    )
    row_totals, col_totals = lax.fori_loop(0, group_limit, group_step, start_totals)
    return (row_totals.reshape(-1, vec_width), col_totals.reshape(-1, vec_width))


def per_device(vectors, blocks, block_rows, block_cols, block_count, lower_edge, upper_edge):
    center = (upper_edge[0] + lower_edge[0]) * 0.5
    half_width = (upper_edge[0] - lower_edge[0]) * 0.5
    local_blocks = blocks[0, 0]
    local_rows = block_rows[0, 0]
    local_cols = block_cols[0, 0]
    slot_count = block_count[0, 0]
    group_size = min(64, local_blocks.shape[0])
    group_limit = local_blocks.shape[0] // group_size
    current = vectors.astype(jnp.float32)
    previous = jnp.zeros_like(current)
    for degree in range(DEGREE):
        operand = current.astype(jnp.bfloat16)
        cols_side = lax.all_gather(operand, "row", axis=0, tiled=True)
        rows_side = lax.all_gather(operand, "col", axis=0, tiled=True)
        row_part, col_part = slot_products(
            local_blocks,
            local_rows,
            local_cols,
            slot_count,
            rows_side,
            cols_side,
            group_size,
            group_limit,
        )
        forward = lax.psum_scatter(row_part, "col", scatter_dimension=0, tiled=True)
        applied = forward + lax.psum_scatter(col_part, "row", scatter_dimension=0, tiled=True)
        shifted = applied - center * current
        if degree == 0:
            following = shifted / half_width
        else:
            following = 2.0 * shifted / half_width - previous
        previous, current = (current, following)
    return current


def densify_kernel(rows_ref, cols_ref, count_ref, blocks_ref, dense_ref, head, follow):
    col_segs, row_segs, seg, _ = dense_ref.shape
    block = blocks_ref.shape[1]
    per_seg = seg // block
    col_blocks = row_segs * per_seg
    count = count_ref[0, 0]

    def clear_head(i, carry):
        head[i] = -1
        return carry

    lax.fori_loop(0, head.shape[0], clear_head, 0, unroll=8)

    def link(i, carry):
        slot = count - 1 - i
        place = rows_ref[slot] * col_blocks + cols_ref[slot]
        follow[slot] = head[place]
        head[place] = slot
        return carry

    lax.fori_loop(0, count, link, 0)

    def clear(i, carry):
        dense_ref[i // row_segs, i % row_segs] = jnp.zeros((seg, seg), dense_ref.dtype)
        return carry

    lax.fori_loop(0, col_segs * row_segs, clear, 0)

    def place_slot(slot, carry):
        row, col = rows_ref[slot], cols_ref[slot]
        after = follow[slot]
        is_first = head[row * col_blocks + col] == slot
        target = dense_ref.at[
            row // per_seg,
            col // per_seg,
            pl.ds(pl.multiple_of((row % per_seg) * block, block), block),
            pl.ds(pl.multiple_of((col % per_seg) * block, block), block),
        ]

        @pl.when(is_first & (after < 0))
        def _():
            target[...] = blocks_ref[slot]

        @pl.when(is_first & (after >= 0))
        def _():
            def more(state):
                return state[0] >= 0

            def add(state):
                at, total = state
                return follow[at], total + blocks_ref[at].astype(jnp.float32)

            _, total = lax.while_loop(more, add, (after, blocks_ref[slot].astype(jnp.float32)))
            target[...] = total.astype(dense_ref.dtype)

        return carry

    lax.fori_loop(0, count, place_slot, 0)


def densify(blocks, block_rows, block_cols, block_count, row_segs, col_segs, seg):
    slots, block, _ = blocks.shape
    places = col_segs * row_segs * (seg // block) ** 2
    return pl.pallas_call(
        densify_kernel,
        out_shape=jax.ShapeDtypeStruct((col_segs, row_segs, seg, seg), jnp.bfloat16),
        in_specs=[pl.BlockSpec(memory_space=pltpu.SMEM)] * 3 + [pl.BlockSpec(memory_space=pltpu.VMEM)],
        out_specs=pl.BlockSpec(memory_space=pltpu.VMEM),
        scratch_shapes=[pltpu.SMEM((places,), jnp.int32), pltpu.SMEM((slots,), jnp.int32)],
        compiler_params=pltpu.CompilerParams(vmem_limit_bytes=48 * 2**20),
        name="densify",
    )(block_rows, block_cols, block_count, blocks)


GATHER = (
    (0, None, 1), (0, None, 2), (0, None, 4),
    (2, 0, 4), (4, 1, 2),
    (2, None, 1), (4, None, 1),
    (6, 0, 1), (6, 1, 1),
)


def filter_kernel(
    n_row, n_col, x_ref, lower_ref, upper_ref, dense_hbm, out_ref,
    dense, rows, cols, mirror_t, forward, current, previous,
    core_out, core_in, diag_out, diag_in, quad_out, quad_in,
    up_out, up_in, down_out, down_in,
    dense_sem, gather_send, gather_recv, chain_up_send, chain_down_send, chain_recv,
    core_send, core_recv, diag_send, diag_recv, quad_send, quad_recv,
    up_send, up_recv, down_send, down_recv,
):
    seg = x_ref.shape[0]
    half = seg // 2
    halves = (pl.ds(0, half), pl.ds(half, half))
    f32, bf16 = jnp.float32, jnp.bfloat16
    r = lax.axis_index("row")
    c = lax.axis_index("col")
    core, along_x, along_y = c % 2, (c // 2) % 2, c // 4
    has_up, has_down = r < n_row - 1, r > 0

    def peer(j):
        y = 1 - along_y if j & 4 else along_y
        x = 1 - along_x if j & 2 else along_x
        k = 1 - core if j & 1 else core
        return y * 4 + x * 2 + k

    def send(src, dst, send_sem, recv_sem, device):
        return pltpu.make_async_remote_copy(
            src_ref=src, dst_ref=dst, send_sem=send_sem, recv_sem=recv_sem,
            device_id=device, device_id_type=MESH,
        )

    def dense_copy(j):
        return pltpu.make_async_copy(dense_hbm.at[peer(j)], dense.at[peer(j)], dense_sem.at[j])

    for j in range(n_col):
        dense_copy(j).start()

    barrier = pltpu.get_barrier_semaphore()
    for j in (1, 2, 4):
        pl.semaphore_signal(barrier, inc=1, device_id=(r, peer(j)), device_id_type=MESH)

    @pl.when(has_up)
    def _():
        pl.semaphore_signal(barrier, inc=1, device_id=(r + 1, c), device_id_type=MESH)

    @pl.when(has_down)
    def _():
        pl.semaphore_signal(barrier, inc=1, device_id=(r - 1, c), device_id_type=MESH)

    pl.semaphore_wait(barrier, 3 + jnp.where(has_up, 1, 0) + jnp.where(has_down, 1, 0))

    center = (upper_ref[0] + lower_ref[0]) * 0.5
    half_width = (upper_ref[0] - lower_ref[0]) * 0.5

    def gather(g, i):
        slot, part, to = GATHER[i]
        src, dst = rows.at[g, slot], rows.at[g, slot ^ to]
        if part is not None:
            src, dst = src.at[halves[part]], dst.at[halves[part]]
        return send(src, dst, gather_send.at[g, i], gather_recv.at[g, i], (r, peer(to)))

    def chain_up(g, q):
        return send(cols.at[g, q], cols.at[g, q], chain_up_send.at[g, q], chain_recv.at[g, q], (r + 1, c))

    def chain_down(g, q):
        return send(cols.at[g, q], cols.at[g, q], chain_down_send.at[g, q], chain_recv.at[g, q], (r - 1, c))

    def sum_up(g, s):
        return send(up_out.at[g, s], up_in.at[g, s], up_send.at[g, s], up_recv.at[g, s], (r + 1, c))

    def sum_down(g, s):
        return send(down_out.at[g, s], down_in.at[g, s], down_send.at[g, s], down_recv.at[g, s], (r - 1, c))

    def core_copy(g, j):
        i = j // 2
        return send(core_out.at[g, i], core_in.at[g, i], core_send.at[g, i], core_recv.at[g, i], (r, peer(1)))

    def diag_copy(g, i):
        return send(diag_out.at[g, i], diag_in.at[g, i], diag_send.at[g, i], diag_recv.at[g, i], (r, peer((2, 4)[i])))

    def quad_copy(g, i, part):
        return send(
            quad_out.at[g, i, halves[part]], quad_in.at[g, i, halves[part]],
            quad_send.at[g, i, part], quad_recv.at[g, i, part], (r, peer((2, 4)[i])),
        )

    def mirror_step(g, j):
        if g == 0:
            dense_copy(j).wait()
        a = peer(j)
        turned = rows[g, j].T

        def one(s, carry):
            product = jnp.dot(turned, dense[a, s], preferred_element_type=f32)
            if j == 0:
                mirror_t[s] = product
            else:
                mirror_t[s] += product
            return carry

        lax.fori_loop(0, n_row, one, 0)

    def forward_step(g, q, first=False):
        def one(a, carry):
            product = jnp.dot(dense[a, q], cols[g, q], preferred_element_type=f32)
            if first:
                forward[a] = product
            else:
                forward[a] += product
            return carry

        lax.fori_loop(0, n_col, one, 0)

    def mirror_of(s):
        return mirror_t[s].T

    def chain_arrive(g, d):
        @pl.when(r >= d)
        def _():
            chain_up(g, r - d).wait_recv()

            @pl.when(has_up)
            def _():
                chain_up(g, r - d).start()

        @pl.when(r < n_row - d)
        def _():
            chain_down(g, r + d).wait_recv()

            @pl.when(has_down)
            def _():
                chain_down(g, r + d).start()

    def chain_use(g, d):
        @pl.when(r >= d)
        def _():
            forward_step(g, r - d)

        @pl.when(r < n_row - d)
        def _():
            forward_step(g, r + d)

    def sum_hop(g, t):
        @pl.when(has_down & has_up & (r <= t))
        def _():
            s = r + n_row - 1 - t
            sum_up(g, s).wait_recv()
            up_out[g, s] = (mirror_of(s) + up_in[g, s].astype(f32)).astype(bf16)
            sum_up(g, s).start()

        @pl.when(has_down & has_up & (n_row - 1 - r <= t))
        def _():
            s = t - (n_row - 1 - r)
            sum_down(g, s).wait_recv()
            down_out[g, s] = (mirror_of(s) + down_in[g, s].astype(f32)).astype(bf16)
            sum_down(g, s).start()

    current[...] = x_ref[...].astype(f32)
    for g in range(DEGREE):
        operand = current[...].astype(bf16)
        rows[g, 0] = operand
        cols[g, r] = operand

        @pl.when(has_up)
        def _():
            chain_up(g, r).start()

        @pl.when(has_down)
        def _():
            chain_down(g, r).start()

        for i in (1, 2, 0):
            gather(g, i).start()
        mirror_step(g, 0)
        gather(g, 0).wait_recv()
        mirror_step(g, 1)
        for i, onward in ((1, (3, 5)), (2, (4, 6))):
            gather(g, i).wait_recv()
            for k in onward:
                gather(g, k).start()
        chain_arrive(g, 1)
        for i, j in ((None, 2), (None, 4), (5, 3), (6, 5)):
            if i is not None:
                gather(g, i).wait_recv()
            mirror_step(g, j)
        for i, onward in ((3, 7), (4, 8)):
            gather(g, i).wait_recv()
            gather(g, onward).start()
        mirror_step(g, 6)
        gather(g, 7).wait_recv()
        gather(g, 8).wait_recv()
        mirror_step(g, 7)

        @pl.when(r == 0)
        def _():
            for s in range(n_row - 1, 0, -1):
                up_out[g, s] = mirror_of(s).astype(bf16)
                sum_up(g, s).start()

        @pl.when(r == n_row - 1)
        def _():
            for s in range(n_row - 1):
                down_out[g, s] = mirror_of(s).astype(bf16)
                sum_down(g, s).start()

        forward_step(g, r, first=True)
        chain_use(g, 1)
        for d in range(2, n_row):
            chain_arrive(g, d)
            chain_use(g, d)

        for j in (7, 3, 5, 1):
            core_out[g, j // 2] = forward[peer(j)].astype(bf16)
            core_copy(g, j).start()
        sum_hop(g, 1)

        def paired(j):
            return forward[peer(j)] + core_in[g, j // 2].astype(f32)

        core_copy(g, 7).wait_recv()
        total = paired(6).astype(bf16)
        for i in (0, 1):
            diag_out[g, i] = total[i * half:(i + 1) * half]
            diag_copy(g, i).start()
        for i, j, free in ((0, 2, 0), (1, 4, 1)):
            core_copy(g, j + 1).wait_recv()
            forward[peer(j)] = paired(j)
            quad_out[g, i, halves[free]] = forward[peer(j), halves[free]].astype(bf16)
            quad_copy(g, i, free).start()
        for i, j, late, source in ((1, 4, 0, 0), (0, 2, 1, 1)):
            diag_copy(g, source).wait_recv()
            quad_out[g, i, halves[late]] = (
                forward[peer(j), halves[late]] + diag_in[g, source].astype(f32)
            ).astype(bf16)
            quad_copy(g, i, late).start()

        for t in range(2, n_row - 1):
            sum_hop(g, t)
        core_copy(g, 1).wait_recv()
        forward[c] = paired(0) + mirror_of(r)
        for i in (0, 1):
            for part in (0, 1):
                quad_copy(g, i, part).wait_recv()
        forward[c] += quad_in[g, 0].astype(f32) + quad_in[g, 1].astype(f32)

        @pl.when(has_down)
        def _():
            sum_up(g, r).wait_recv()
            forward[c] += up_in[g, r].astype(f32)

        @pl.when(has_up)
        def _():
            sum_down(g, r).wait_recv()
            forward[c] += down_in[g, r].astype(f32)

        shifted = forward[c] - center * current[...]
        if g == 0:
            following = shifted / half_width
        else:
            following = 2.0 * shifted / half_width - previous[...]
        if g == DEGREE - 1:
            out_ref[...] = following
        else:
            previous[...] = current[...]
            current[...] = following

    for g in range(DEGREE):
        for i in range(len(GATHER)):
            gather(g, i).wait_send()
        for j in (1, 3, 5, 7):
            core_copy(g, j).wait_send()
        for i in (0, 1):
            diag_copy(g, i).wait_send()
            for part in (0, 1):
                quad_copy(g, i, part).wait_send()
        for q in range(n_row):
            @pl.when(has_up & (q <= r))
            def _():
                chain_up(g, q).wait_send()

            @pl.when(has_down & (q >= r))
            def _():
                chain_down(g, q).wait_send()

            @pl.when(q > r)
            def _():
                sum_up(g, q).wait_send()

            @pl.when(q < r)
            def _():
                sum_down(g, q).wait_send()


def filter_call(vectors, lower_edge, upper_edge, dense, n_row, n_col):
    seg, width = vectors.shape
    half = seg // 2
    f32, bf16 = jnp.float32, jnp.bfloat16
    vmem, dma = pltpu.VMEM, pltpu.SemaphoreType.DMA
    g = DEGREE
    scratch = [
        vmem(dense.shape, bf16),
        vmem((g, n_col, seg, width), bf16),
        vmem((g, n_row, seg, width), bf16),
        vmem((n_row, width, seg), f32),
        vmem((n_col, seg, width), f32),
        vmem((seg, width), f32),
        vmem((seg, width), f32),
        vmem((g, n_col // 2, seg, width), bf16),
        vmem((g, n_col // 2, seg, width), bf16),
        vmem((g, 2, half, width), bf16),
        vmem((g, 2, half, width), bf16),
        vmem((g, 2, seg, width), bf16),
        vmem((g, 2, seg, width), bf16),
    ]
    scratch += [vmem((g, n_row, seg, width), bf16)] * 4
    scratch += [dma((n_col,))] + [dma((g, len(GATHER)))] * 2 + [dma((g, n_row))] * 3
    scratch += [dma((g, n_col // 2))] * 2 + [dma((g, 2))] * 2 + [dma((g, 2, 2))] * 2
    scratch += [dma((g, n_row))] * 4
    return pl.pallas_call(
        functools.partial(filter_kernel, n_row, n_col),
        out_shape=jax.ShapeDtypeStruct((seg, width), f32),
        in_specs=[
            pl.BlockSpec(memory_space=pltpu.VMEM),
            pl.BlockSpec(memory_space=pltpu.SMEM),
            pl.BlockSpec(memory_space=pltpu.SMEM),
            pl.BlockSpec(memory_space=pl.ANY),
        ],
        out_specs=pl.BlockSpec(memory_space=pltpu.VMEM),
        scratch_shapes=scratch,
        compiler_params=pltpu.CompilerParams(
            collective_id=0, has_side_effects=True, vmem_limit_bytes=56 * 2**20
        ),
        name="filter",
    )(vectors, lower_edge, upper_edge, dense)


def per_device_dense(
    n_row, n_col, vectors, blocks, block_rows, block_cols, block_count, lower_edge, upper_edge
):
    dense = densify(
        blocks[0, 0], block_rows[0, 0], block_cols[0, 0], block_count, n_row, n_col, vectors.shape[0]
    )
    return filter_call(vectors, lower_edge, upper_edge, dense, n_row, n_col)


def per_device_any(n_row, n_col, vectors, *others):
    dense_bytes = 2 * n_row * n_col * vectors.shape[0] ** 2
    if n_col == 8 and n_row >= 2 and dense_bytes <= 16 * 2**20:
        return per_device_dense(n_row, n_col, vectors, *others)
    return per_device(vectors, *others)


def solution(mesh):
    return jax.shard_map(
        functools.partial(per_device_any, mesh.shape["row"], mesh.shape["col"]),
        mesh=mesh,
        in_specs=(
            P(("row", "col"), None),
            P("row", "col", None, None, None),
            P("row", "col", None),
            P("row", "col", None),
            P("row", "col"),
            P(),
            P(),
        ),
        out_specs=P(("row", "col"), None),
        check_vma=False,
    )
```

```python
import functools

import jax
import jax.numpy as jnp
from jax import lax
from jax.experimental import pallas as pl
from jax.experimental.pallas import tpu as pltpu
from jax.sharding import PartitionSpec as P

MESH = pl.DeviceIdType.MESH

DEGREE = 2


def pick_table(indices, count):
    return (indices[:, None] == jnp.arange(count, dtype=jnp.int32)[None, :]).astype(jnp.bfloat16)


def place_sum(table, values):
    upper = values.astype(jnp.bfloat16)
    lower = (values - upper.astype(jnp.float32)).astype(jnp.bfloat16)
    first = jnp.einsum("gt,giv->tiv", table, upper, preferred_element_type=jnp.float32)
    second = jnp.einsum("gt,giv->tiv", table, lower, preferred_element_type=jnp.float32)
    return first + second


def slot_products(
    local_blocks, local_rows, local_cols, slot_count, rows_side, cols_side, group_size, group_limit
):
    block_size = local_blocks.shape[1]
    vec_width = rows_side.shape[1]
    row_tiles = rows_side.reshape(-1, block_size, vec_width)
    col_tiles = cols_side.reshape(-1, block_size, vec_width)
    row_count = row_tiles.shape[0]
    col_count = col_tiles.shape[0]

    def group_step(position, totals):
        row_totals, col_totals = totals
        first_slot = position * group_size
        block_tile = lax.dynamic_slice_in_dim(local_blocks, first_slot, group_size, 0)
        rows_here = lax.dynamic_slice_in_dim(local_rows, first_slot, group_size, 0)
        cols_here = lax.dynamic_slice_in_dim(local_cols, first_slot, group_size, 0)
        live_mask = (first_slot + jnp.arange(group_size) < slot_count).astype(jnp.float32)[
            :, None, None
        ]
        row_table = pick_table(rows_here, row_count)
        col_table = pick_table(cols_here, col_count)
        col_picked = jnp.einsum(
            "gt,tjv->gjv", col_table, col_tiles, preferred_element_type=jnp.float32
        ).astype(jnp.bfloat16)
        row_picked = jnp.einsum(
            "gt,tjv->gjv", row_table, row_tiles, preferred_element_type=jnp.float32
        ).astype(jnp.bfloat16)
        forward = (
            jnp.einsum("gij,gjv->giv", block_tile, col_picked, preferred_element_type=jnp.float32)
            * live_mask
        )
        mirror = (
            jnp.einsum("gji,gjv->giv", block_tile, row_picked, preferred_element_type=jnp.float32)
            * live_mask
        )
        return (
            row_totals + place_sum(row_table, forward),
            col_totals + place_sum(col_table, mirror),
        )

    start_totals = (
        jnp.zeros(row_tiles.shape, jnp.float32),
        jnp.zeros(col_tiles.shape, jnp.float32),
    )
    row_totals, col_totals = lax.fori_loop(0, group_limit, group_step, start_totals)
    return (row_totals.reshape(-1, vec_width), col_totals.reshape(-1, vec_width))


def per_device(vectors, blocks, block_rows, block_cols, block_count, lower_edge, upper_edge):
    center = (upper_edge[0] + lower_edge[0]) * 0.5
    half_width = (upper_edge[0] - lower_edge[0]) * 0.5
    local_blocks = blocks[0, 0]
    local_rows = block_rows[0, 0]
    local_cols = block_cols[0, 0]
    slot_count = block_count[0, 0]
    group_size = min(64, local_blocks.shape[0])
    group_limit = local_blocks.shape[0] // group_size
    current = vectors.astype(jnp.float32)
    previous = jnp.zeros_like(current)
    for degree in range(DEGREE):
        operand = current.astype(jnp.bfloat16)
        cols_side = lax.all_gather(operand, "row", axis=0, tiled=True)
        rows_side = lax.all_gather(operand, "col", axis=0, tiled=True)
        row_part, col_part = slot_products(
            local_blocks,
            local_rows,
            local_cols,
            slot_count,
            rows_side,
            cols_side,
            group_size,
            group_limit,
        )
        forward = lax.psum_scatter(row_part, "col", scatter_dimension=0, tiled=True)
        applied = forward + lax.psum_scatter(col_part, "row", scatter_dimension=0, tiled=True)
        shifted = applied - center * current
        if degree == 0:
            following = shifted / half_width
        else:
            following = 2.0 * shifted / half_width - previous
        previous, current = (current, following)
    return current


def link_kernel(
    col_blocks, rows_ref, cols_ref, count_ref, blocks_hbm, table_ref, sums_ref, held, follow, repeats, sem
):
    slots = blocks_hbm.shape[2]
    empty = follow.shape[0] - 1
    count = count_ref[0, 0]
    load = pltpu.make_async_copy(blocks_hbm.at[0, 0], held, sem)
    load.start()

    def clear(i, carry):
        for k in range(16):
            table_ref[i * 16 + k] = empty
        return carry

    lax.fori_loop(0, table_ref.shape[0] // 16, clear, 0)
    follow[empty] = -1

    def link(slot, found):
        place = rows_ref[0, 0, slot] * col_blocks + cols_ref[0, 0, slot]
        before = table_ref[place]
        follow[slot] = before
        table_ref[place] = slot
        repeats[found] = place
        return found + jnp.where(follow[before] == empty, 1, 0)

    found = lax.fori_loop(0, count, link, 0)
    load.wait()

    def sum_place(i, carry):
        place = repeats[i]
        last = table_ref[place]

        def more(state):
            return state[0] != empty

        def add(state):
            at, total = state
            return follow[at], total + held[at].astype(jnp.float32)

        _, total = lax.while_loop(more, add, (follow[last], held[last].astype(jnp.float32)))
        sums_ref[i] = total.astype(sums_ref.dtype)
        table_ref[place] = slots + i
        return carry

    lax.fori_loop(0, found, sum_place, 0)


def link_call(blocks, block_rows, block_cols, block_count, row_blocks, col_blocks):
    _, _, slots, block, _ = blocks.shape
    sums = slots // 2
    smem = pl.BlockSpec(memory_space=pltpu.SMEM)
    return pl.pallas_call(
        functools.partial(link_kernel, col_blocks),
        out_shape=(
            jax.ShapeDtypeStruct((row_blocks * col_blocks,), jnp.int32),
            jax.ShapeDtypeStruct((sums, block, block), jnp.bfloat16),
        ),
        in_specs=[smem] * 3 + [pl.BlockSpec(memory_space=pl.ANY)],
        out_specs=(smem, pl.BlockSpec(memory_space=pltpu.VMEM)),
        scratch_shapes=[
            pltpu.VMEM((slots, block, block), jnp.bfloat16),
            pltpu.SMEM((slots + sums + 1,), jnp.int32),
            pltpu.SMEM((slots + 1,), jnp.int32),
            pltpu.SemaphoreType.DMA,
        ],
        compiler_params=pltpu.CompilerParams(vmem_limit_bytes=62 * 2**20),
        name="link",
    )(block_rows, block_cols, block_count, blocks)


GATHER = (
    (0, None, 1), (0, None, 2), (0, None, 4),
    (2, 0, 4), (4, 1, 2),
    (2, None, 1), (4, None, 1),
    (6, 0, 1), (6, 1, 1),
)


def filter_kernel(
    n_row, n_col, x_ref, lower_ref, upper_ref, table_ref, blocks_hbm, sums_hbm, out_ref,
    pool, dense, rows, cols, mirror_t, forward, current, previous,
    core_out, core_in, diag_out, diag_in, quad_out, quad_in,
    up_out, up_in, down_out, down_in,
    pool_sem, gather_send, gather_recv, chain_up_send, chain_down_send, chain_recv,
    core_send, core_recv, diag_send, diag_recv, quad_send, quad_recv,
    up_send, up_recv, down_send, down_recv,
):
    seg = x_ref.shape[0]
    half = seg // 2
    halves = (pl.ds(0, half), pl.ds(half, half))
    f32, bf16 = jnp.float32, jnp.bfloat16
    r = lax.axis_index("row")
    c = lax.axis_index("col")
    core, along_x, along_y = c % 2, (c // 2) % 2, c // 4
    has_up, has_down = r < n_row - 1, r > 0

    def peer(j):
        y = 1 - along_y if j & 4 else along_y
        x = 1 - along_x if j & 2 else along_x
        k = 1 - core if j & 1 else core
        return y * 4 + x * 2 + k

    def send(src, dst, send_sem, recv_sem, device):
        return pltpu.make_async_remote_copy(
            src_ref=src, dst_ref=dst, send_sem=send_sem, recv_sem=recv_sem,
            device_id=device, device_id_type=MESH,
        )

    slots, sums = blocks_hbm.shape[2], sums_hbm.shape[0]
    loads = (
        pltpu.make_async_copy(blocks_hbm.at[0, 0], pool.at[pl.ds(0, slots)], pool_sem.at[0]),
        pltpu.make_async_copy(sums_hbm, pool.at[pl.ds(slots, sums)], pool_sem.at[1]),
    )
    for load in loads:
        load.start()
    pool[slots + sums] = jnp.zeros(pool.shape[1:], pool.dtype)

    barrier = pltpu.get_barrier_semaphore()
    for j in (1, 2, 4):
        pl.semaphore_signal(barrier, inc=1, device_id=(r, peer(j)), device_id_type=MESH)

    @pl.when(has_up)
    def _():
        pl.semaphore_signal(barrier, inc=1, device_id=(r + 1, c), device_id_type=MESH)

    @pl.when(has_down)
    def _():
        pl.semaphore_signal(barrier, inc=1, device_id=(r - 1, c), device_id_type=MESH)

    pl.semaphore_wait(barrier, 3 + jnp.where(has_up, 1, 0) + jnp.where(has_down, 1, 0))

    center = (upper_ref[0] + lower_ref[0]) * 0.5
    half_width = (upper_ref[0] - lower_ref[0]) * 0.5

    def gather(g, i):
        slot, part, to = GATHER[i]
        src, dst = rows.at[g, slot], rows.at[g, slot ^ to]
        if part is not None:
            src, dst = src.at[halves[part]], dst.at[halves[part]]
        return send(src, dst, gather_send.at[g, i], gather_recv.at[g, i], (r, peer(to)))

    def chain_up(g, q):
        return send(cols.at[g, q], cols.at[g, q], chain_up_send.at[g, q], chain_recv.at[g, q], (r + 1, c))

    def chain_down(g, q):
        return send(cols.at[g, q], cols.at[g, q], chain_down_send.at[g, q], chain_recv.at[g, q], (r - 1, c))

    def sum_up(g, s):
        return send(up_out.at[g, s], up_in.at[g, s], up_send.at[g, s], up_recv.at[g, s], (r + 1, c))

    def sum_down(g, s):
        return send(down_out.at[g, s], down_in.at[g, s], down_send.at[g, s], down_recv.at[g, s], (r - 1, c))

    def core_copy(g, j):
        i = j // 2
        return send(core_out.at[g, i], core_in.at[g, i], core_send.at[g, i], core_recv.at[g, i], (r, peer(1)))

    def diag_copy(g, i):
        return send(diag_out.at[g, i], diag_in.at[g, i], diag_send.at[g, i], diag_recv.at[g, i], (r, peer((2, 4)[i])))

    def quad_copy(g, i, part):
        return send(
            quad_out.at[g, i, halves[part]], quad_in.at[g, i, halves[part]],
            quad_send.at[g, i, part], quad_recv.at[g, i, part], (r, peer((2, 4)[i])),
        )

    block = pool.shape[1]
    per_seg = seg // block

    def assemble(a):
        def one(i, carry):
            row, s = i // n_row, i % n_row
            first = ((a * per_seg + row) * n_row + s) * per_seg
            for k in range(per_seg):
                dense[
                    a, s, pl.ds(pl.multiple_of(row * block, block), block), pl.ds(k * block, block)
                ] = pool[table_ref[first + k]]
            return carry

        lax.fori_loop(0, per_seg * n_row, one, 0)

    def mirror_step(g, j):
        a = peer(j)
        if g == 0:
            assemble(a)
        turned = rows[g, j].T

        def one(s, carry):
            product = jnp.dot(turned, dense[a, s], preferred_element_type=f32)
            if j == 0:
                mirror_t[s] = product
            else:
                mirror_t[s] += product
            return carry

        lax.fori_loop(0, n_row, one, 0)

    def forward_step(g, q, first=False):
        def one(a, carry):
            product = jnp.dot(dense[a, q], cols[g, q], preferred_element_type=f32)
            if first:
                forward[a] = product
            else:
                forward[a] += product
            return carry

        lax.fori_loop(0, n_col, one, 0)

    q_last = jnp.where(2 * r < n_row, n_row - 1, 0)

    def forward_last(g, j):
        a = peer(j)
        forward[a] += jnp.dot(dense[a, q_last], cols[g, q_last], preferred_element_type=f32)

    def mirror_of(s):
        return mirror_t[s].T

    def chain_arrive(g, d):
        @pl.when(r >= d)
        def _():
            chain_up(g, r - d).wait_recv()

            @pl.when(has_up)
            def _():
                chain_up(g, r - d).start()

        @pl.when(r < n_row - d)
        def _():
            chain_down(g, r + d).wait_recv()

            @pl.when(has_down)
            def _():
                chain_down(g, r + d).start()

    def chain_use(g, d):
        @pl.when((r >= d) & (r - d != q_last))
        def _():
            forward_step(g, r - d)

        @pl.when((r < n_row - d) & (r + d != q_last))
        def _():
            forward_step(g, r + d)

    def sum_hop(g, t):
        @pl.when(has_down & has_up & (r <= t))
        def _():
            s = r + n_row - 1 - t
            sum_up(g, s).wait_recv()
            up_out[g, s] = (mirror_of(s) + up_in[g, s].astype(f32)).astype(bf16)
            sum_up(g, s).start()

        @pl.when(has_down & has_up & (n_row - 1 - r <= t))
        def _():
            s = t - (n_row - 1 - r)
            sum_down(g, s).wait_recv()
            down_out[g, s] = (mirror_of(s) + down_in[g, s].astype(f32)).astype(bf16)
            sum_down(g, s).start()

    current[...] = x_ref[...].astype(f32)
    for g in range(DEGREE):
        operand = current[...].astype(bf16)
        rows[g, 0] = operand
        cols[g, r] = operand

        @pl.when(has_up)
        def _():
            chain_up(g, r).start()

        @pl.when(has_down)
        def _():
            chain_down(g, r).start()

        for i in (1, 2, 0):
            gather(g, i).start()
        if g == 0:
            for load in loads:
                load.wait()
        mirror_step(g, 0)
        gather(g, 0).wait_recv()
        mirror_step(g, 1)
        for i, onward in ((1, (3, 5)), (2, (4, 6))):
            gather(g, i).wait_recv()
            for k in onward:
                gather(g, k).start()
        chain_arrive(g, 1)
        for i, j in ((None, 2), (None, 4), (5, 3), (6, 5)):
            if i is not None:
                gather(g, i).wait_recv()
            mirror_step(g, j)
        for i, onward in ((3, 7), (4, 8)):
            gather(g, i).wait_recv()
            gather(g, onward).start()
        mirror_step(g, 6)
        if n_row > 2:
            chain_arrive(g, 2)
        gather(g, 7).wait_recv()
        gather(g, 8).wait_recv()
        mirror_step(g, 7)

        @pl.when(r == 0)
        def _():
            for s in range(n_row - 1, 0, -1):
                up_out[g, s] = mirror_of(s).astype(bf16)
                sum_up(g, s).start()

        @pl.when(r == n_row - 1)
        def _():
            for s in range(n_row - 1):
                down_out[g, s] = mirror_of(s).astype(bf16)
                sum_down(g, s).start()

        forward_step(g, r, first=True)
        chain_use(g, 1)
        for d in range(2, n_row):
            if d > 2:
                chain_arrive(g, d)
            chain_use(g, d)

        for j in (7, 3, 5, 1):
            forward_last(g, j)
            core_out[g, j // 2] = forward[peer(j)].astype(bf16)
            core_copy(g, j).start()
        for j in (6, 2, 4, 0):
            forward_last(g, j)

        def paired(j):
            return forward[peer(j)] + core_in[g, j // 2].astype(f32)

        core_copy(g, 7).wait_recv()
        total = paired(6).astype(bf16)
        for i in (0, 1):
            diag_out[g, i] = total[i * half:(i + 1) * half]
            diag_copy(g, i).start()
        for i, j, free in ((0, 2, 0), (1, 4, 1)):
            core_copy(g, j + 1).wait_recv()
            forward[peer(j)] = paired(j)
            quad_out[g, i, halves[free]] = forward[peer(j), halves[free]].astype(bf16)
            quad_copy(g, i, free).start()
        sum_hop(g, 1)
        for i, j, late, source in ((1, 4, 0, 0), (0, 2, 1, 1)):
            diag_copy(g, source).wait_recv()
            quad_out[g, i, halves[late]] = (
                forward[peer(j), halves[late]] + diag_in[g, source].astype(f32)
            ).astype(bf16)
            quad_copy(g, i, late).start()

        for t in range(2, n_row - 1):
            sum_hop(g, t)
        core_copy(g, 1).wait_recv()
        forward[c] = paired(0) + mirror_of(r)
        for i in (0, 1):
            for part in (0, 1):
                quad_copy(g, i, part).wait_recv()
        forward[c] += quad_in[g, 0].astype(f32) + quad_in[g, 1].astype(f32)

        @pl.when(has_down)
        def _():
            sum_up(g, r).wait_recv()
            forward[c] += up_in[g, r].astype(f32)

        @pl.when(has_up)
        def _():
            sum_down(g, r).wait_recv()
            forward[c] += down_in[g, r].astype(f32)

        shifted = forward[c] - center * current[...]
        if g == 0:
            following = shifted / half_width
        else:
            following = 2.0 * shifted / half_width - previous[...]
        if g == DEGREE - 1:
            out_ref[...] = following
        else:
            previous[...] = current[...]
            current[...] = following

    for g in range(DEGREE):
        for i in range(len(GATHER)):
            gather(g, i).wait_send()
        for j in (1, 3, 5, 7):
            core_copy(g, j).wait_send()
        for i in (0, 1):
            diag_copy(g, i).wait_send()
            for part in (0, 1):
                quad_copy(g, i, part).wait_send()
        for q in range(n_row):
            @pl.when(has_up & (q <= r))
            def _():
                chain_up(g, q).wait_send()

            @pl.when(has_down & (q >= r))
            def _():
                chain_down(g, q).wait_send()

            @pl.when(q > r)
            def _():
                sum_up(g, q).wait_send()

            @pl.when(q < r)
            def _():
                sum_down(g, q).wait_send()


def filter_call(vectors, lower_edge, upper_edge, table, blocks, sums, n_row, n_col):
    seg, width = vectors.shape
    half = seg // 2
    f32, bf16 = jnp.float32, jnp.bfloat16
    vmem, dma = pltpu.VMEM, pltpu.SemaphoreType.DMA
    g = DEGREE
    scratch = [
        vmem((blocks.shape[2] + sums.shape[0] + 1,) + sums.shape[1:], bf16),
        vmem((n_col, n_row, seg, seg), bf16),
        vmem((g, n_col, seg, width), bf16),
        vmem((g, n_row, seg, width), bf16),
        vmem((n_row, width, seg), f32),
        vmem((n_col, seg, width), f32),
        vmem((seg, width), f32),
        vmem((seg, width), f32),
        vmem((g, n_col // 2, seg, width), bf16),
        vmem((g, n_col // 2, seg, width), bf16),
        vmem((g, 2, half, width), bf16),
        vmem((g, 2, half, width), bf16),
        vmem((g, 2, seg, width), bf16),
        vmem((g, 2, seg, width), bf16),
    ]
    scratch += [vmem((g, n_row, seg, width), bf16)] * 4
    scratch += [dma((2,))] + [dma((g, len(GATHER)))] * 2 + [dma((g, n_row))] * 3
    scratch += [dma((g, n_col // 2))] * 2 + [dma((g, 2))] * 2 + [dma((g, 2, 2))] * 2
    scratch += [dma((g, n_row))] * 4
    return pl.pallas_call(
        functools.partial(filter_kernel, n_row, n_col),
        out_shape=jax.ShapeDtypeStruct((seg, width), f32),
        in_specs=[
            pl.BlockSpec(memory_space=pltpu.VMEM),
            pl.BlockSpec(memory_space=pltpu.SMEM),
            pl.BlockSpec(memory_space=pltpu.SMEM),
            pl.BlockSpec(memory_space=pltpu.SMEM),
            pl.BlockSpec(memory_space=pl.ANY),
            pl.BlockSpec(memory_space=pl.ANY),
        ],
        out_specs=pl.BlockSpec(memory_space=pltpu.VMEM),
        scratch_shapes=scratch,
        compiler_params=pltpu.CompilerParams(
            collective_id=0, has_side_effects=True, vmem_limit_bytes=62 * 2**20
        ),
        name="filter",
    )(vectors, lower_edge, upper_edge, table, blocks, sums)


def per_device_dense(
    n_row, n_col, vectors, blocks, block_rows, block_cols, block_count, lower_edge, upper_edge
):
    per_seg = vectors.shape[0] // blocks.shape[-1]
    table, sums = link_call(
        blocks, block_rows, block_cols, block_count, n_col * per_seg, n_row * per_seg
    )
    return filter_call(vectors, lower_edge, upper_edge, table, blocks, sums, n_row, n_col)


def per_device_any(n_row, n_col, vectors, *others):
    dense_bytes = 2 * n_row * n_col * vectors.shape[0] ** 2
    if n_col == 8 and n_row >= 2 and dense_bytes <= 16 * 2**20:
        return per_device_dense(n_row, n_col, vectors, *others)
    return per_device(vectors, *others)


def solution(mesh):
    return jax.shard_map(
        functools.partial(per_device_any, mesh.shape["row"], mesh.shape["col"]),
        mesh=mesh,
        in_specs=(
            P(("row", "col"), None),
            P("row", "col", None, None, None),
            P("row", "col", None),
            P("row", "col", None),
            P("row", "col"),
            P(),
            P(),
        ),
        out_specs=P(("row", "col"), None),
        check_vma=False,
    )
```

```python
import functools

import jax
import jax.numpy as jnp
from jax import lax
from jax.experimental import pallas as pl
from jax.experimental.pallas import tpu as pltpu
from jax.sharding import PartitionSpec as P

MESH = pl.DeviceIdType.MESH

DEGREE = 2


def pick_table(indices, count):
    return (indices[:, None] == jnp.arange(count, dtype=jnp.int32)[None, :]).astype(jnp.bfloat16)


def place_sum(table, values):
    upper = values.astype(jnp.bfloat16)
    lower = (values - upper.astype(jnp.float32)).astype(jnp.bfloat16)
    first = jnp.einsum("gt,giv->tiv", table, upper, preferred_element_type=jnp.float32)
    second = jnp.einsum("gt,giv->tiv", table, lower, preferred_element_type=jnp.float32)
    return first + second


def slot_products(
    local_blocks, local_rows, local_cols, slot_count, rows_side, cols_side, group_size, group_limit
):
    block_size = local_blocks.shape[1]
    vec_width = rows_side.shape[1]
    row_tiles = rows_side.reshape(-1, block_size, vec_width)
    col_tiles = cols_side.reshape(-1, block_size, vec_width)
    row_count = row_tiles.shape[0]
    col_count = col_tiles.shape[0]

    def group_step(position, totals):
        row_totals, col_totals = totals
        first_slot = position * group_size
        block_tile = lax.dynamic_slice_in_dim(local_blocks, first_slot, group_size, 0)
        rows_here = lax.dynamic_slice_in_dim(local_rows, first_slot, group_size, 0)
        cols_here = lax.dynamic_slice_in_dim(local_cols, first_slot, group_size, 0)
        live_mask = (first_slot + jnp.arange(group_size) < slot_count).astype(jnp.float32)[
            :, None, None
        ]
        row_table = pick_table(rows_here, row_count)
        col_table = pick_table(cols_here, col_count)
        col_picked = jnp.einsum(
            "gt,tjv->gjv", col_table, col_tiles, preferred_element_type=jnp.float32
        ).astype(jnp.bfloat16)
        row_picked = jnp.einsum(
            "gt,tjv->gjv", row_table, row_tiles, preferred_element_type=jnp.float32
        ).astype(jnp.bfloat16)
        forward = (
            jnp.einsum("gij,gjv->giv", block_tile, col_picked, preferred_element_type=jnp.float32)
            * live_mask
        )
        mirror = (
            jnp.einsum("gji,gjv->giv", block_tile, row_picked, preferred_element_type=jnp.float32)
            * live_mask
        )
        return (
            row_totals + place_sum(row_table, forward),
            col_totals + place_sum(col_table, mirror),
        )

    start_totals = (
        jnp.zeros(row_tiles.shape, jnp.float32),
        jnp.zeros(col_tiles.shape, jnp.float32),
    )
    row_totals, col_totals = lax.fori_loop(0, group_limit, group_step, start_totals)
    return (row_totals.reshape(-1, vec_width), col_totals.reshape(-1, vec_width))


def per_device(vectors, blocks, block_rows, block_cols, block_count, lower_edge, upper_edge):
    center = (upper_edge[0] + lower_edge[0]) * 0.5
    half_width = (upper_edge[0] - lower_edge[0]) * 0.5
    local_blocks = blocks[0, 0]
    local_rows = block_rows[0, 0]
    local_cols = block_cols[0, 0]
    slot_count = block_count[0, 0]
    group_size = min(64, local_blocks.shape[0])
    group_limit = local_blocks.shape[0] // group_size
    current = vectors.astype(jnp.float32)
    previous = jnp.zeros_like(current)
    for degree in range(DEGREE):
        operand = current.astype(jnp.bfloat16)
        cols_side = lax.all_gather(operand, "row", axis=0, tiled=True)
        rows_side = lax.all_gather(operand, "col", axis=0, tiled=True)
        row_part, col_part = slot_products(
            local_blocks,
            local_rows,
            local_cols,
            slot_count,
            rows_side,
            cols_side,
            group_size,
            group_limit,
        )
        forward = lax.psum_scatter(row_part, "col", scatter_dimension=0, tiled=True)
        applied = forward + lax.psum_scatter(col_part, "row", scatter_dimension=0, tiled=True)
        shifted = applied - center * current
        if degree == 0:
            following = shifted / half_width
        else:
            following = 2.0 * shifted / half_width - previous
        previous, current = (current, following)
    return current


def link_kernel(
    col_blocks, rows_ref, cols_ref, count_ref, blocks_hbm, table_ref, sums_ref, held, follow, repeats, sem
):
    slots = blocks_hbm.shape[2]
    empty = follow.shape[0] - 1
    count = count_ref[0, 0]
    load = pltpu.make_async_copy(blocks_hbm.at[0, 0], held, sem)
    load.start()

    def clear(i, carry):
        for k in range(16):
            table_ref[i * 16 + k] = empty
        return carry

    lax.fori_loop(0, table_ref.shape[0] // 16, clear, 0)
    follow[empty] = -1

    def link(slot, found):
        place = rows_ref[0, 0, slot] * col_blocks + cols_ref[0, 0, slot]
        before = table_ref[place]
        follow[slot] = before
        table_ref[place] = slot
        repeats[found] = place
        return found + jnp.where(follow[before] == empty, 1, 0)

    found = lax.fori_loop(0, count, link, 0)
    load.wait()

    def sum_place(i, carry):
        place = repeats[i]
        last = table_ref[place]

        def more(state):
            return state[0] != empty

        def add(state):
            at, total = state
            return follow[at], total + held[at].astype(jnp.float32)

        _, total = lax.while_loop(more, add, (follow[last], held[last].astype(jnp.float32)))
        sums_ref[i] = total.astype(sums_ref.dtype)
        table_ref[place] = slots + i
        return carry

    lax.fori_loop(0, found, sum_place, 0)


def link_call(blocks, block_rows, block_cols, block_count, row_blocks, col_blocks):
    _, _, slots, block, _ = blocks.shape
    sums = slots // 2
    smem = pl.BlockSpec(memory_space=pltpu.SMEM)
    return pl.pallas_call(
        functools.partial(link_kernel, col_blocks),
        out_shape=(
            jax.ShapeDtypeStruct((row_blocks * col_blocks,), jnp.int32),
            jax.ShapeDtypeStruct((sums, block, block), jnp.bfloat16),
        ),
        in_specs=[smem] * 3 + [pl.BlockSpec(memory_space=pl.ANY)],
        out_specs=(smem, pl.BlockSpec(memory_space=pltpu.VMEM)),
        scratch_shapes=[
            pltpu.VMEM((slots, block, block), jnp.bfloat16),
            pltpu.SMEM((slots + sums + 1,), jnp.int32),
            pltpu.SMEM((slots + 1,), jnp.int32),
            pltpu.SemaphoreType.DMA,
        ],
        compiler_params=pltpu.CompilerParams(vmem_limit_bytes=62 * 2**20),
        name="link",
    )(block_rows, block_cols, block_count, blocks)


GATHER = (
    (0, None, 1), (0, 0, 2), (0, 1, 4), (0, 1, 2), (0, 0, 4),
    (2, 0, 4), (4, 1, 2),
    (2, None, 1), (4, None, 1),
    (6, 0, 1), (6, 1, 1),
)


def filter_kernel(
    n_row, n_col, x_ref, lower_ref, upper_ref, table_ref, blocks_hbm, sums_hbm, out_ref,
    pool, dense, rows, cols, mirror_t, forward, current, previous,
    core_out, core_in, diag_out, diag_in, quad_out, quad_in,
    up_out, up_in, down_out, down_in,
    pool_sem, gather_send, gather_recv, chain_up_send, chain_down_send, chain_recv,
    core_send, core_recv, diag_send, diag_recv, quad_send, quad_recv,
    up_send, up_recv, down_send, down_recv,
):
    seg = x_ref.shape[0]
    half = seg // 2
    halves = (pl.ds(0, half), pl.ds(half, half))
    f32, bf16 = jnp.float32, jnp.bfloat16
    r = lax.axis_index("row")
    c = lax.axis_index("col")
    core, along_x, along_y = c % 2, (c // 2) % 2, c // 4
    has_up, has_down = r < n_row - 1, r > 0

    def peer(j):
        y = 1 - along_y if j & 4 else along_y
        x = 1 - along_x if j & 2 else along_x
        k = 1 - core if j & 1 else core
        return y * 4 + x * 2 + k

    def send(src, dst, send_sem, recv_sem, device):
        return pltpu.make_async_remote_copy(
            src_ref=src, dst_ref=dst, send_sem=send_sem, recv_sem=recv_sem,
            device_id=device, device_id_type=MESH,
        )

    slots, sums = blocks_hbm.shape[2], sums_hbm.shape[0]
    loads = (
        pltpu.make_async_copy(blocks_hbm.at[0, 0], pool.at[pl.ds(0, slots)], pool_sem.at[0]),
        pltpu.make_async_copy(sums_hbm, pool.at[pl.ds(slots, sums)], pool_sem.at[1]),
    )
    for load in loads:
        load.start()
    pool[slots + sums] = jnp.zeros(pool.shape[1:], pool.dtype)

    barrier = pltpu.get_barrier_semaphore()
    for j in (1, 2, 4):
        pl.semaphore_signal(barrier, inc=1, device_id=(r, peer(j)), device_id_type=MESH)

    @pl.when(has_up)
    def _():
        pl.semaphore_signal(barrier, inc=1, device_id=(r + 1, c), device_id_type=MESH)

    @pl.when(has_down)
    def _():
        pl.semaphore_signal(barrier, inc=1, device_id=(r - 1, c), device_id_type=MESH)

    pl.semaphore_wait(barrier, 3 + jnp.where(has_up, 1, 0) + jnp.where(has_down, 1, 0))

    center = (upper_ref[0] + lower_ref[0]) * 0.5
    half_width = (upper_ref[0] - lower_ref[0]) * 0.5

    def gather(g, i):
        slot, part, to = GATHER[i]
        src, dst = rows.at[g, slot], rows.at[g, slot ^ to]
        if part is not None:
            src, dst = src.at[halves[part]], dst.at[halves[part]]
        return send(src, dst, gather_send.at[g, i], gather_recv.at[g, i], (r, peer(to)))

    def chain_up(g, q, p):
        part = cols.at[g, q, halves[p]]
        return send(part, part, chain_up_send.at[g, q, p], chain_recv.at[g, q, p], (r + 1, c))

    def chain_down(g, q, p):
        part = cols.at[g, q, halves[p]]
        return send(part, part, chain_down_send.at[g, q, p], chain_recv.at[g, q, p], (r - 1, c))

    def sum_up(g, s, p):
        return send(
            up_out.at[g, s, halves[p]], up_in.at[g, s, halves[p]],
            up_send.at[g, s, p], up_recv.at[g, s, p], (r + 1, c),
        )

    def sum_down(g, s, p):
        return send(
            down_out.at[g, s, halves[p]], down_in.at[g, s, halves[p]],
            down_send.at[g, s, p], down_recv.at[g, s, p], (r - 1, c),
        )

    def core_copy(g, j):
        i = j // 2
        return send(core_out.at[g, i], core_in.at[g, i], core_send.at[g, i], core_recv.at[g, i], (r, peer(1)))

    def diag_copy(g, i):
        return send(diag_out.at[g, i], diag_in.at[g, i], diag_send.at[g, i], diag_recv.at[g, i], (r, peer((2, 4)[i])))

    def quad_copy(g, i, part):
        return send(
            quad_out.at[g, i, halves[part]], quad_in.at[g, i, halves[part]],
            quad_send.at[g, i, part], quad_recv.at[g, i, part], (r, peer((2, 4)[i])),
        )

    block = pool.shape[1]
    per_seg = seg // block

    def assemble(a):
        def one(i, carry):
            row, s = i // n_row, i % n_row
            first = ((a * per_seg + row) * n_row + s) * per_seg
            for k in range(per_seg):
                dense[
                    a, s, pl.ds(pl.multiple_of(row * block, block), block), pl.ds(k * block, block)
                ] = pool[table_ref[first + k]]
            return carry

        lax.fori_loop(0, per_seg * n_row, one, 0)

    def mirror_step(g, j):
        a = peer(j)
        if g == 0:
            assemble(a)
        turned = rows[g, j].T

        def one(s, carry):
            product = jnp.dot(turned, dense[a, s], preferred_element_type=f32)
            if j == 0:
                mirror_t[s] = product
            else:
                mirror_t[s] += product
            return carry

        lax.fori_loop(0, n_row, one, 0)

    def forward_step(g, q, first=False):
        def one(a, carry):
            product = jnp.dot(dense[a, q], cols[g, q], preferred_element_type=f32)
            if first:
                forward[a] = product
            else:
                forward[a] += product
            return carry

        lax.fori_loop(0, n_col, one, 0)

    q_last = jnp.where(2 * r < n_row, n_row - 1, 0)

    def forward_last(g, j):
        a = peer(j)
        forward[a] += jnp.dot(dense[a, q_last], cols[g, q_last], preferred_element_type=f32)

    def mirror_of(s, p):
        return mirror_t[s, :, halves[p]].T

    def mirror_last(g, j):
        a = peer(j)
        if g == 0:
            assemble(a)
        turned = rows[g, j].T
        for i in range(n_row):
            s = jnp.where(2 * r < n_row, n_row - 1 - i, i)
            mirror_t[s] += jnp.dot(turned, dense[a, s], preferred_element_type=f32)
            if i == n_row - 1:
                break

            @pl.when(r == 0)
            def _():
                for p in (0, 1):
                    up_out[g, n_row - 1 - i, halves[p]] = mirror_of(n_row - 1 - i, p).astype(bf16)
                    sum_up(g, n_row - 1 - i, p).start()

            @pl.when(r == n_row - 1)
            def _():
                for p in (0, 1):
                    down_out[g, i, halves[p]] = mirror_of(i, p).astype(bf16)
                    sum_down(g, i, p).start()

    def chain_arrive(g, d, p):
        @pl.when(r >= d)
        def _():
            chain_up(g, r - d, p).wait_recv()

            @pl.when(has_up)
            def _():
                chain_up(g, r - d, p).start()

        @pl.when(r < n_row - d)
        def _():
            chain_down(g, r + d, p).wait_recv()

            @pl.when(has_down)
            def _():
                chain_down(g, r + d, p).start()

    def chain_use(g, d):
        @pl.when((r >= d) & (r - d != q_last))
        def _():
            forward_step(g, r - d)

        @pl.when((r < n_row - d) & (r + d != q_last))
        def _():
            forward_step(g, r + d)

    def sum_hop(g, t, p):
        @pl.when(has_down & has_up & (r <= t))
        def _():
            s = r + n_row - 1 - t
            sum_up(g, s, p).wait_recv()
            up_out[g, s, halves[p]] = (mirror_of(s, p) + up_in[g, s, halves[p]].astype(f32)).astype(bf16)
            sum_up(g, s, p).start()

        @pl.when(has_down & has_up & (n_row - 1 - r <= t))
        def _():
            s = t - (n_row - 1 - r)
            sum_down(g, s, p).wait_recv()
            down_out[g, s, halves[p]] = (mirror_of(s, p) + down_in[g, s, halves[p]].astype(f32)).astype(bf16)
            sum_down(g, s, p).start()

    current[...] = x_ref[...].astype(f32)
    for g in range(DEGREE):
        operand = current[...].astype(bf16)
        rows[g, 0] = operand
        cols[g, r] = operand

        @pl.when(has_up)
        def _():
            for p in (0, 1):
                chain_up(g, r, p).start()

        @pl.when(has_down)
        def _():
            for p in (0, 1):
                chain_down(g, r, p).start()

        for i in (1, 2, 3, 4, 0):
            gather(g, i).start()
        if g == 0:
            for load in loads:
                load.wait()
        mirror_step(g, 0)
        gather(g, 0).wait_recv()
        mirror_step(g, 1)
        for i, onward in ((1, 5), (2, 6)):
            gather(g, i).wait_recv()
            gather(g, onward).start()
        chain_arrive(g, 1, 0)
        if g > 0:
            forward_step(g, r, first=True)
        for i, onward in ((3, 7), (4, 8)):
            gather(g, i).wait_recv()
            gather(g, onward).start()
        chain_arrive(g, 1, 1)
        mirror_step(g, 2)
        mirror_step(g, 4)
        for i, onward in ((5, 9), (6, 10)):
            gather(g, i).wait_recv()
            gather(g, onward).start()
        if n_row > 2:
            chain_arrive(g, 2, 0)
        for i, j in ((7, 3), (8, 5)):
            gather(g, i).wait_recv()
            mirror_step(g, j)
        mirror_step(g, 6)
        if n_row > 2:
            chain_arrive(g, 2, 1)
        gather(g, 9).wait_recv()
        gather(g, 10).wait_recv()
        mirror_last(g, 7)
        if g == 0:
            forward_step(g, r, first=True)
        chain_use(g, 1)
        for d in range(2, n_row):
            if d > 2:
                for p in (0, 1):
                    chain_arrive(g, d, p)
            chain_use(g, d)

        for j in (7, 3, 5, 1):
            forward_last(g, j)
            core_out[g, j // 2] = forward[peer(j)].astype(bf16)
            core_copy(g, j).start()
        for j in (6, 2, 4, 0):
            forward_last(g, j)
        if n_row > 2:
            sum_hop(g, 1, 0)

        def paired(j):
            return forward[peer(j)] + core_in[g, j // 2].astype(f32)

        core_copy(g, 7).wait_recv()
        total = paired(6).astype(bf16)
        for i in (0, 1):
            diag_out[g, i] = total[i * half:(i + 1) * half]
            diag_copy(g, i).start()
        for i, j, free in ((0, 2, 0), (1, 4, 1)):
            core_copy(g, j + 1).wait_recv()
            forward[peer(j)] = paired(j)
            quad_out[g, i, halves[free]] = forward[peer(j), halves[free]].astype(bf16)
            quad_copy(g, i, free).start()
        if n_row > 2:
            sum_hop(g, 1, 1)
        for i, j, late, source in ((1, 4, 0, 0), (0, 2, 1, 1)):
            diag_copy(g, source).wait_recv()
            quad_out[g, i, halves[late]] = (
                forward[peer(j), halves[late]] + diag_in[g, source].astype(f32)
            ).astype(bf16)
            quad_copy(g, i, late).start()

        for t in range(2, n_row - 1):
            for p in (0, 1):
                sum_hop(g, t, p)
        core_copy(g, 1).wait_recv()
        forward[c] = paired(0)
        for p in (0, 1):
            forward[c, halves[p]] += mirror_of(r, p)
        for i in (0, 1):
            for part in (0, 1):
                quad_copy(g, i, part).wait_recv()
        forward[c] += quad_in[g, 0].astype(f32) + quad_in[g, 1].astype(f32)

        @pl.when(has_down)
        def _():
            for p in (0, 1):
                sum_up(g, r, p).wait_recv()
                forward[c, halves[p]] += up_in[g, r, halves[p]].astype(f32)

        @pl.when(has_up)
        def _():
            for p in (0, 1):
                sum_down(g, r, p).wait_recv()
                forward[c, halves[p]] += down_in[g, r, halves[p]].astype(f32)

        shifted = forward[c] - center * current[...]
        if g == 0:
            following = shifted / half_width
        else:
            following = 2.0 * shifted / half_width - previous[...]
        if g == DEGREE - 1:
            out_ref[...] = following
        else:
            previous[...] = current[...]
            current[...] = following

    for g in range(DEGREE):
        for i in range(len(GATHER)):
            gather(g, i).wait_send()
        for j in (1, 3, 5, 7):
            core_copy(g, j).wait_send()
        for i in (0, 1):
            diag_copy(g, i).wait_send()
            for part in (0, 1):
                quad_copy(g, i, part).wait_send()
        for q in range(n_row):
            @pl.when(has_up & (q <= r))
            def _():
                for p in (0, 1):
                    chain_up(g, q, p).wait_send()

            @pl.when(has_down & (q >= r))
            def _():
                for p in (0, 1):
                    chain_down(g, q, p).wait_send()

            @pl.when(q > r)
            def _():
                for p in (0, 1):
                    sum_up(g, q, p).wait_send()

            @pl.when(q < r)
            def _():
                for p in (0, 1):
                    sum_down(g, q, p).wait_send()


def filter_call(vectors, lower_edge, upper_edge, table, blocks, sums, n_row, n_col):
    seg, width = vectors.shape
    half = seg // 2
    f32, bf16 = jnp.float32, jnp.bfloat16
    vmem, dma = pltpu.VMEM, pltpu.SemaphoreType.DMA
    g = DEGREE
    scratch = [
        vmem((blocks.shape[2] + sums.shape[0] + 1,) + sums.shape[1:], bf16),
        vmem((n_col, n_row, seg, seg), bf16),
        vmem((g, n_col, seg, width), bf16),
        vmem((g, n_row, seg, width), bf16),
        vmem((n_row, width, seg), f32),
        vmem((n_col, seg, width), f32),
        vmem((seg, width), f32),
        vmem((seg, width), f32),
        vmem((g, n_col // 2, seg, width), bf16),
        vmem((g, n_col // 2, seg, width), bf16),
        vmem((g, 2, half, width), bf16),
        vmem((g, 2, half, width), bf16),
        vmem((g, 2, seg, width), bf16),
        vmem((g, 2, seg, width), bf16),
    ]
    scratch += [vmem((g, n_row, seg, width), bf16)] * 4
    scratch += [dma((2,))] + [dma((g, len(GATHER)))] * 2 + [dma((g, n_row, 2))] * 3
    scratch += [dma((g, n_col // 2))] * 2 + [dma((g, 2))] * 2 + [dma((g, 2, 2))] * 2
    scratch += [dma((g, n_row, 2))] * 4
    return pl.pallas_call(
        functools.partial(filter_kernel, n_row, n_col),
        out_shape=jax.ShapeDtypeStruct((seg, width), f32),
        in_specs=[
            pl.BlockSpec(memory_space=pltpu.VMEM),
            pl.BlockSpec(memory_space=pltpu.SMEM),
            pl.BlockSpec(memory_space=pltpu.SMEM),
            pl.BlockSpec(memory_space=pltpu.SMEM),
            pl.BlockSpec(memory_space=pl.ANY),
            pl.BlockSpec(memory_space=pl.ANY),
        ],
        out_specs=pl.BlockSpec(memory_space=pltpu.VMEM),
        scratch_shapes=scratch,
        compiler_params=pltpu.CompilerParams(
            collective_id=0, has_side_effects=True, vmem_limit_bytes=62 * 2**20
        ),
        name="filter",
    )(vectors, lower_edge, upper_edge, table, blocks, sums)


def per_device_dense(
    n_row, n_col, vectors, blocks, block_rows, block_cols, block_count, lower_edge, upper_edge
):
    per_seg = vectors.shape[0] // blocks.shape[-1]
    table, sums = link_call(
        blocks, block_rows, block_cols, block_count, n_col * per_seg, n_row * per_seg
    )
    return filter_call(vectors, lower_edge, upper_edge, table, blocks, sums, n_row, n_col)


def per_device_any(n_row, n_col, vectors, *others):
    dense_bytes = 2 * n_row * n_col * vectors.shape[0] ** 2
    if n_col == 8 and n_row >= 2 and dense_bytes <= 16 * 2**20:
        return per_device_dense(n_row, n_col, vectors, *others)
    return per_device(vectors, *others)


def solution(mesh):
    return jax.shard_map(
        functools.partial(per_device_any, mesh.shape["row"], mesh.shape["col"]),
        mesh=mesh,
        in_specs=(
            P(("row", "col"), None),
            P("row", "col", None, None, None),
            P("row", "col", None),
            P("row", "col", None),
            P("row", "col"),
            P(),
            P(),
        ),
        out_specs=P(("row", "col"), None),
        check_vma=False,
    )
```

```python
import functools

import jax
import jax.numpy as jnp
from jax import lax
from jax.experimental import pallas as pl
from jax.experimental.pallas import tpu as pltpu
from jax.sharding import PartitionSpec as P

MESH = pl.DeviceIdType.MESH

DEGREE = 2


def pick_table(indices, count):
    return (indices[:, None] == jnp.arange(count, dtype=jnp.int32)[None, :]).astype(jnp.bfloat16)


def place_sum(table, values):
    upper = values.astype(jnp.bfloat16)
    lower = (values - upper.astype(jnp.float32)).astype(jnp.bfloat16)
    first = jnp.einsum("gt,giv->tiv", table, upper, preferred_element_type=jnp.float32)
    second = jnp.einsum("gt,giv->tiv", table, lower, preferred_element_type=jnp.float32)
    return first + second


def slot_products(
    local_blocks, local_rows, local_cols, slot_count, rows_side, cols_side, group_size, group_limit
):
    block_size = local_blocks.shape[1]
    vec_width = rows_side.shape[1]
    row_tiles = rows_side.reshape(-1, block_size, vec_width)
    col_tiles = cols_side.reshape(-1, block_size, vec_width)
    row_count = row_tiles.shape[0]
    col_count = col_tiles.shape[0]

    def group_step(position, totals):
        row_totals, col_totals = totals
        first_slot = position * group_size
        block_tile = lax.dynamic_slice_in_dim(local_blocks, first_slot, group_size, 0)
        rows_here = lax.dynamic_slice_in_dim(local_rows, first_slot, group_size, 0)
        cols_here = lax.dynamic_slice_in_dim(local_cols, first_slot, group_size, 0)
        live_mask = (first_slot + jnp.arange(group_size) < slot_count).astype(jnp.float32)[
            :, None, None
        ]
        row_table = pick_table(rows_here, row_count)
        col_table = pick_table(cols_here, col_count)
        col_picked = jnp.einsum(
            "gt,tjv->gjv", col_table, col_tiles, preferred_element_type=jnp.float32
        ).astype(jnp.bfloat16)
        row_picked = jnp.einsum(
            "gt,tjv->gjv", row_table, row_tiles, preferred_element_type=jnp.float32
        ).astype(jnp.bfloat16)
        forward = (
            jnp.einsum("gij,gjv->giv", block_tile, col_picked, preferred_element_type=jnp.float32)
            * live_mask
        )
        mirror = (
            jnp.einsum("gji,gjv->giv", block_tile, row_picked, preferred_element_type=jnp.float32)
            * live_mask
        )
        return (
            row_totals + place_sum(row_table, forward),
            col_totals + place_sum(col_table, mirror),
        )

    start_totals = (
        jnp.zeros(row_tiles.shape, jnp.float32),
        jnp.zeros(col_tiles.shape, jnp.float32),
    )
    row_totals, col_totals = lax.fori_loop(0, group_limit, group_step, start_totals)
    return (row_totals.reshape(-1, vec_width), col_totals.reshape(-1, vec_width))


def per_device(vectors, blocks, block_rows, block_cols, block_count, lower_edge, upper_edge):
    center = (upper_edge[0] + lower_edge[0]) * 0.5
    half_width = (upper_edge[0] - lower_edge[0]) * 0.5
    local_blocks = blocks[0, 0]
    local_rows = block_rows[0, 0]
    local_cols = block_cols[0, 0]
    slot_count = block_count[0, 0]
    group_size = min(64, local_blocks.shape[0])
    group_limit = local_blocks.shape[0] // group_size
    current = vectors.astype(jnp.float32)
    previous = jnp.zeros_like(current)
    for degree in range(DEGREE):
        operand = current.astype(jnp.bfloat16)
        cols_side = lax.all_gather(operand, "row", axis=0, tiled=True)
        rows_side = lax.all_gather(operand, "col", axis=0, tiled=True)
        row_part, col_part = slot_products(
            local_blocks,
            local_rows,
            local_cols,
            slot_count,
            rows_side,
            cols_side,
            group_size,
            group_limit,
        )
        forward = lax.psum_scatter(row_part, "col", scatter_dimension=0, tiled=True)
        applied = forward + lax.psum_scatter(col_part, "row", scatter_dimension=0, tiled=True)
        shifted = applied - center * current
        if degree == 0:
            following = shifted / half_width
        else:
            following = 2.0 * shifted / half_width - previous
        previous, current = (current, following)
    return current


def link_kernel(
    col_blocks, rows_ref, cols_ref, count_ref, blocks_hbm, table_ref, sums_ref, held, follow, repeats, sem
):
    slots = blocks_hbm.shape[2]
    empty = follow.shape[0] - 1
    count = count_ref[0, 0]
    load = pltpu.make_async_copy(blocks_hbm.at[0, 0], held, sem)
    load.start()

    def clear(i, carry):
        for k in range(16):
            table_ref[i * 16 + k] = empty
        return carry

    lax.fori_loop(0, table_ref.shape[0] // 16, clear, 0)
    follow[empty] = -1

    def link(slot, found):
        place = rows_ref[0, 0, slot] * col_blocks + cols_ref[0, 0, slot]
        before = table_ref[place]
        follow[slot] = before
        table_ref[place] = slot
        repeats[found] = place
        return found + jnp.where(follow[before] == empty, 1, 0)

    found = lax.fori_loop(0, count, link, 0)
    load.wait()

    def sum_place(i, carry):
        place = repeats[i]
        last = table_ref[place]

        def more(state):
            return state[0] != empty

        def add(state):
            at, total = state
            return follow[at], total + held[at].astype(jnp.float32)

        _, total = lax.while_loop(more, add, (follow[last], held[last].astype(jnp.float32)))
        sums_ref[i] = total.astype(sums_ref.dtype)
        table_ref[place] = slots + i
        return carry

    lax.fori_loop(0, found, sum_place, 0)


def link_call(blocks, block_rows, block_cols, block_count, row_blocks, col_blocks):
    _, _, slots, block, _ = blocks.shape
    sums = slots // 2
    smem = pl.BlockSpec(memory_space=pltpu.SMEM)
    return pl.pallas_call(
        functools.partial(link_kernel, col_blocks),
        out_shape=(
            jax.ShapeDtypeStruct((row_blocks * col_blocks,), jnp.int32),
            jax.ShapeDtypeStruct((sums, block, block), jnp.bfloat16),
        ),
        in_specs=[smem] * 3 + [pl.BlockSpec(memory_space=pl.ANY)],
        out_specs=(smem, pl.BlockSpec(memory_space=pltpu.VMEM)),
        scratch_shapes=[
            pltpu.VMEM((slots, block, block), jnp.bfloat16),
            pltpu.SMEM((slots + sums + 1,), jnp.int32),
            pltpu.SMEM((slots + 1,), jnp.int32),
            pltpu.SemaphoreType.DMA,
        ],
        compiler_params=pltpu.CompilerParams(vmem_limit_bytes=62 * 2**20),
        name="link",
    )(block_rows, block_cols, block_count, blocks)


GATHER = (
    (0, None, 1), (0, 0, 2), (0, 1, 4), (0, 1, 2), (0, 0, 4),
    (2, 0, 4), (4, 1, 2),
    (2, None, 1), (4, None, 1),
    (6, 0, 1), (6, 1, 1),
)


def filter_kernel(
    n_row, n_col, x_ref, lower_ref, upper_ref, table_ref, blocks_hbm, sums_hbm, out_ref,
    pool, dense, rows, cols, mirror_t, forward, current, previous,
    core_out, core_in, diag_out, diag_in, quad_out, quad_in,
    up_out, up_in, down_out, down_in,
    pool_sem, gather_send, gather_recv, chain_up_send, chain_down_send, chain_recv,
    core_send, core_recv, diag_send, diag_recv, quad_send, quad_recv,
    up_send, up_recv, down_send, down_recv,
):
    seg = x_ref.shape[0]
    half = seg // 2
    halves = (pl.ds(0, half), pl.ds(half, half))
    f32, bf16 = jnp.float32, jnp.bfloat16
    r = lax.axis_index("row")
    c = lax.axis_index("col")
    core, along_x, along_y = c % 2, (c // 2) % 2, c // 4
    has_up, has_down = r < n_row - 1, r > 0

    def peer(j):
        y = 1 - along_y if j & 4 else along_y
        x = 1 - along_x if j & 2 else along_x
        k = 1 - core if j & 1 else core
        return y * 4 + x * 2 + k

    def send(src, dst, send_sem, recv_sem, device):
        return pltpu.make_async_remote_copy(
            src_ref=src, dst_ref=dst, send_sem=send_sem, recv_sem=recv_sem,
            device_id=device, device_id_type=MESH,
        )

    slots, sums = blocks_hbm.shape[2], sums_hbm.shape[0]
    loads = (
        pltpu.make_async_copy(blocks_hbm.at[0, 0], pool.at[pl.ds(0, slots)], pool_sem.at[0]),
        pltpu.make_async_copy(sums_hbm, pool.at[pl.ds(slots, sums)], pool_sem.at[1]),
    )
    for load in loads:
        load.start()
    pool[slots + sums] = jnp.zeros(pool.shape[1:], pool.dtype)

    barrier = pltpu.get_barrier_semaphore()
    for j in (1, 2, 4):
        pl.semaphore_signal(barrier, inc=1, device_id=(r, peer(j)), device_id_type=MESH)

    @pl.when(has_up)
    def _():
        pl.semaphore_signal(barrier, inc=1, device_id=(r + 1, c), device_id_type=MESH)

    @pl.when(has_down)
    def _():
        pl.semaphore_signal(barrier, inc=1, device_id=(r - 1, c), device_id_type=MESH)

    pl.semaphore_wait(barrier, 3 + jnp.where(has_up, 1, 0) + jnp.where(has_down, 1, 0))

    center = (upper_ref[0] + lower_ref[0]) * 0.5
    half_width = (upper_ref[0] - lower_ref[0]) * 0.5

    def gather(g, i):
        slot, part, to = GATHER[i]
        src, dst = rows.at[g, slot], rows.at[g, slot ^ to]
        if part is not None:
            src, dst = src.at[halves[part]], dst.at[halves[part]]
        return send(src, dst, gather_send.at[g, i], gather_recv.at[g, i], (r, peer(to)))

    def chain_up(g, q, p):
        part = cols.at[g, q, halves[p]]
        return send(part, part, chain_up_send.at[g, q, p], chain_recv.at[g, q, p], (r + 1, c))

    def chain_down(g, q, p):
        part = cols.at[g, q, halves[p]]
        return send(part, part, chain_down_send.at[g, q, p], chain_recv.at[g, q, p], (r - 1, c))

    def sum_up(g, s, p):
        return send(
            up_out.at[g, s, halves[p]], up_in.at[g, s, halves[p]],
            up_send.at[g, s, p], up_recv.at[g, s, p], (r + 1, c),
        )

    def sum_down(g, s, p):
        return send(
            down_out.at[g, s, halves[p]], down_in.at[g, s, halves[p]],
            down_send.at[g, s, p], down_recv.at[g, s, p], (r - 1, c),
        )

    def core_copy(g, j):
        i = j // 2
        return send(core_out.at[g, i], core_in.at[g, i], core_send.at[g, i], core_recv.at[g, i], (r, peer(1)))

    def diag_copy(g, i):
        return send(diag_out.at[g, i], diag_in.at[g, i], diag_send.at[g, i], diag_recv.at[g, i], (r, peer((2, 4)[i])))

    def quad_copy(g, i, part):
        return send(
            quad_out.at[g, i, halves[part]], quad_in.at[g, i, halves[part]],
            quad_send.at[g, i, part], quad_recv.at[g, i, part], (r, peer((2, 4)[i])),
        )

    block = pool.shape[1]
    per_seg = seg // block

    def assemble(a):
        def one(i, carry):
            row, s = i // n_row, i % n_row
            first = ((a * per_seg + row) * n_row + s) * per_seg
            for k in range(per_seg):
                dense[
                    a, s, pl.ds(pl.multiple_of(row * block, block), block), pl.ds(k * block, block)
                ] = pool[table_ref[first + k]]
            return carry

        lax.fori_loop(0, per_seg * n_row, one, 0)

    def mirror_step(g, *slots_here):
        segments = [peer(j) for j in slots_here]
        if g == 0:
            for a in segments:
                assemble(a)
        turned = [rows[g, j].T for j in slots_here]

        def one(s, carry):
            product = sum(
                jnp.dot(t, dense[a, s], preferred_element_type=f32) for t, a in zip(turned, segments)
            )
            if 0 in slots_here:
                mirror_t[s] = product
            else:
                mirror_t[s] += product
            return carry

        lax.fori_loop(0, n_row, one, 0)

    def forward_step(g, q, first=False):
        def one(a, carry):
            product = jnp.dot(dense[a, q], cols[g, q], preferred_element_type=f32)
            if first:
                forward[a] = product
            else:
                forward[a] += product
            return carry

        lax.fori_loop(0, n_col, one, 0)

    q_last = jnp.where(2 * r < n_row, n_row - 1, 0)

    def forward_last(g, j):
        a = peer(j)
        forward[a] += jnp.dot(dense[a, q_last], cols[g, q_last], preferred_element_type=f32)

    def mirror_of(s, p):
        return mirror_t[s, :, halves[p]].T

    def mirror_last(g, j):
        a = peer(j)
        if g == 0:
            assemble(a)
        turned = rows[g, j].T
        for i in range(n_row):
            s = jnp.where(2 * r < n_row, n_row - 1 - i, i)
            mirror_t[s] += jnp.dot(turned, dense[a, s], preferred_element_type=f32)
            if i == n_row - 1:
                break

            @pl.when(r == 0)
            def _():
                for p in (0, 1):
                    up_out[g, n_row - 1 - i, halves[p]] = mirror_of(n_row - 1 - i, p).astype(bf16)
                    sum_up(g, n_row - 1 - i, p).start()

            @pl.when(r == n_row - 1)
            def _():
                for p in (0, 1):
                    down_out[g, i, halves[p]] = mirror_of(i, p).astype(bf16)
                    sum_down(g, i, p).start()

    def chain_arrive(g, d, p):
        @pl.when(r >= d)
        def _():
            chain_up(g, r - d, p).wait_recv()

            @pl.when(has_up)
            def _():
                chain_up(g, r - d, p).start()

        @pl.when(r < n_row - d)
        def _():
            chain_down(g, r + d, p).wait_recv()

            @pl.when(has_down)
            def _():
                chain_down(g, r + d, p).start()

    def chain_use(g, d):
        @pl.when((r >= d) & (r - d != q_last))
        def _():
            forward_step(g, r - d)

        @pl.when((r < n_row - d) & (r + d != q_last))
        def _():
            forward_step(g, r + d)

    def sum_hop(g, t, p):
        @pl.when(has_down & has_up & (r <= t))
        def _():
            s = r + n_row - 1 - t
            sum_up(g, s, p).wait_recv()
            up_out[g, s, halves[p]] = (mirror_of(s, p) + up_in[g, s, halves[p]].astype(f32)).astype(bf16)
            sum_up(g, s, p).start()

        @pl.when(has_down & has_up & (n_row - 1 - r <= t))
        def _():
            s = t - (n_row - 1 - r)
            sum_down(g, s, p).wait_recv()
            down_out[g, s, halves[p]] = (mirror_of(s, p) + down_in[g, s, halves[p]].astype(f32)).astype(bf16)
            sum_down(g, s, p).start()

    def begin(g, p):
        @pl.when(has_up)
        def _():
            chain_up(g, r, p).start()

        @pl.when(has_down)
        def _():
            chain_down(g, r, p).start()

        for i in ((1, 4), (3, 2))[p]:
            gather(g, i).start()

    current[...] = x_ref[...].astype(f32)
    rows[0, 0] = x_ref[...]
    cols[0, r] = x_ref[...]
    for p in (0, 1):
        begin(0, p)
    gather(0, 0).start()
    for g in range(DEGREE):
        if g > 0:
            gather(g, 0).wait_recv()
            mirror_step(g, 0, 1)
        for i, onward in ((1, 5), (2, 6)):
            gather(g, i).wait_recv()
            gather(g, onward).start()
        chain_arrive(g, 1, 0)
        if g > 0:
            forward_step(g, r, first=True)
        else:
            for load in loads:
                load.wait()
            gather(g, 0).wait_recv()
            mirror_step(g, 0, 1)
        for i, onward in ((3, 7), (4, 8)):
            gather(g, i).wait_recv()
            gather(g, onward).start()
        chain_arrive(g, 1, 1)
        mirror_step(g, 2, 4)
        for i, onward in ((5, 9), (6, 10)):
            gather(g, i).wait_recv()
            gather(g, onward).start()
        if n_row > 2:
            chain_arrive(g, 2, 0)
        for i in (7, 8):
            gather(g, i).wait_recv()
        mirror_step(g, 3, 5)
        mirror_step(g, 6)
        if n_row > 2:
            chain_arrive(g, 2, 1)
        gather(g, 9).wait_recv()
        gather(g, 10).wait_recv()
        mirror_last(g, 7)
        if g == 0:
            forward_step(g, r, first=True)
        chain_use(g, 1)
        for d in range(2, n_row):
            if d > 2:
                for p in (0, 1):
                    chain_arrive(g, d, p)
            chain_use(g, d)

        for j in (7, 3, 5, 1):
            forward_last(g, j)
            core_out[g, j // 2] = forward[peer(j)].astype(bf16)
            core_copy(g, j).start()
        for j in (6, 2, 4, 0):
            forward_last(g, j)
        if n_row > 2:
            sum_hop(g, 1, 0)

        def paired(j):
            return forward[peer(j)] + core_in[g, j // 2].astype(f32)

        core_copy(g, 7).wait_recv()
        total = paired(6).astype(bf16)
        for i in (0, 1):
            diag_out[g, i] = total[i * half:(i + 1) * half]
            diag_copy(g, i).start()
        for i, j, free in ((0, 2, 0), (1, 4, 1)):
            core_copy(g, j + 1).wait_recv()
            forward[peer(j)] = paired(j)
            quad_out[g, i, halves[free]] = forward[peer(j), halves[free]].astype(bf16)
            quad_copy(g, i, free).start()
        if n_row > 2:
            sum_hop(g, 1, 1)
        for i, j, late, source in ((1, 4, 0, 0), (0, 2, 1, 1)):
            diag_copy(g, source).wait_recv()
            quad_out[g, i, halves[late]] = (
                forward[peer(j), halves[late]] + diag_in[g, source].astype(f32)
            ).astype(bf16)
            quad_copy(g, i, late).start()

        for t in range(2, n_row - 1):
            for p in (0, 1):
                sum_hop(g, t, p)
        core_copy(g, 1).wait_recv()
        for p in (0, 1):
            part = halves[p]
            for i in (0, 1):
                quad_copy(g, i, p).wait_recv()
            forward[c, part] += (
                core_in[g, 0, part].astype(f32) + mirror_of(r, p)
                + (quad_in[g, 0, part].astype(f32) + quad_in[g, 1, part].astype(f32))
            )

            @pl.when(has_down)
            def _():
                sum_up(g, r, p).wait_recv()
                forward[c, part] += up_in[g, r, part].astype(f32)

            @pl.when(has_up)
            def _():
                sum_down(g, r, p).wait_recv()
                forward[c, part] += down_in[g, r, part].astype(f32)

            shifted = forward[c, part] - center * current[part]
            if g == 0:
                following = shifted / half_width
            else:
                following = 2.0 * shifted / half_width - previous[part]
            if g == DEGREE - 1:
                out_ref[part] = following
            else:
                previous[part] = current[part]
                current[part] = following
                rows[g + 1, 0, part] = following.astype(bf16)
                cols[g + 1, r, part] = following.astype(bf16)
                begin(g + 1, p)
        if g < DEGREE - 1:
            gather(g + 1, 0).start()

    for g in range(DEGREE):
        for i in range(len(GATHER)):
            gather(g, i).wait_send()
        for j in (1, 3, 5, 7):
            core_copy(g, j).wait_send()
        for i in (0, 1):
            diag_copy(g, i).wait_send()
            for part in (0, 1):
                quad_copy(g, i, part).wait_send()
        for q in range(n_row):
            @pl.when(has_up & (q <= r))
            def _():
                for p in (0, 1):
                    chain_up(g, q, p).wait_send()

            @pl.when(has_down & (q >= r))
            def _():
                for p in (0, 1):
                    chain_down(g, q, p).wait_send()

            @pl.when(q > r)
            def _():
                for p in (0, 1):
                    sum_up(g, q, p).wait_send()

            @pl.when(q < r)
            def _():
                for p in (0, 1):
                    sum_down(g, q, p).wait_send()


def filter_call(vectors, lower_edge, upper_edge, table, blocks, sums, n_row, n_col):
    seg, width = vectors.shape
    half = seg // 2
    f32, bf16 = jnp.float32, jnp.bfloat16
    vmem, dma = pltpu.VMEM, pltpu.SemaphoreType.DMA
    g = DEGREE
    scratch = [
        vmem((blocks.shape[2] + sums.shape[0] + 1,) + sums.shape[1:], bf16),
        vmem((n_col, n_row, seg, seg), bf16),
        vmem((g, n_col, seg, width), bf16),
        vmem((g, n_row, seg, width), bf16),
        vmem((n_row, width, seg), f32),
        vmem((n_col, seg, width), f32),
        vmem((seg, width), f32),
        vmem((seg, width), f32),
        vmem((g, n_col // 2, seg, width), bf16),
        vmem((g, n_col // 2, seg, width), bf16),
        vmem((g, 2, half, width), bf16),
        vmem((g, 2, half, width), bf16),
        vmem((g, 2, seg, width), bf16),
        vmem((g, 2, seg, width), bf16),
    ]
    scratch += [vmem((g, n_row, seg, width), bf16)] * 4
    scratch += [dma((2,))] + [dma((g, len(GATHER)))] * 2 + [dma((g, n_row, 2))] * 3
    scratch += [dma((g, n_col // 2))] * 2 + [dma((g, 2))] * 2 + [dma((g, 2, 2))] * 2
    scratch += [dma((g, n_row, 2))] * 4
    return pl.pallas_call(
        functools.partial(filter_kernel, n_row, n_col),
        out_shape=jax.ShapeDtypeStruct((seg, width), f32),
        in_specs=[
            pl.BlockSpec(memory_space=pltpu.VMEM),
            pl.BlockSpec(memory_space=pltpu.SMEM),
            pl.BlockSpec(memory_space=pltpu.SMEM),
            pl.BlockSpec(memory_space=pltpu.SMEM),
            pl.BlockSpec(memory_space=pl.ANY),
            pl.BlockSpec(memory_space=pl.ANY),
        ],
        out_specs=pl.BlockSpec(memory_space=pltpu.VMEM),
        scratch_shapes=scratch,
        compiler_params=pltpu.CompilerParams(
            collective_id=0, has_side_effects=True, vmem_limit_bytes=62 * 2**20
        ),
        name="filter",
    )(vectors, lower_edge, upper_edge, table, blocks, sums)


def per_device_dense(
    n_row, n_col, vectors, blocks, block_rows, block_cols, block_count, lower_edge, upper_edge
):
    per_seg = vectors.shape[0] // blocks.shape[-1]
    table, sums = link_call(
        blocks, block_rows, block_cols, block_count, n_col * per_seg, n_row * per_seg
    )
    return filter_call(vectors, lower_edge, upper_edge, table, blocks, sums, n_row, n_col)


def per_device_any(n_row, n_col, vectors, *others):
    dense_bytes = 2 * n_row * n_col * vectors.shape[0] ** 2
    if n_col == 8 and n_row >= 2 and dense_bytes <= 16 * 2**20:
        return per_device_dense(n_row, n_col, vectors, *others)
    return per_device(vectors, *others)


def solution(mesh):
    return jax.shard_map(
        functools.partial(per_device_any, mesh.shape["row"], mesh.shape["col"]),
        mesh=mesh,
        in_specs=(
            P(("row", "col"), None),
            P("row", "col", None, None, None),
            P("row", "col", None),
            P("row", "col", None),
            P("row", "col"),
            P(),
            P(),
        ),
        out_specs=P(("row", "col"), None),
        check_vma=False,
    )
```

```python
import functools

import jax
import jax.numpy as jnp
from jax import lax
from jax.experimental import pallas as pl
from jax.experimental.pallas import tpu as pltpu
from jax.sharding import PartitionSpec as P

MESH = pl.DeviceIdType.MESH

DEGREE = 2


def pick_table(indices, count):
    return (indices[:, None] == jnp.arange(count, dtype=jnp.int32)[None, :]).astype(jnp.bfloat16)


def place_sum(table, values):
    upper = values.astype(jnp.bfloat16)
    lower = (values - upper.astype(jnp.float32)).astype(jnp.bfloat16)
    first = jnp.einsum("gt,giv->tiv", table, upper, preferred_element_type=jnp.float32)
    second = jnp.einsum("gt,giv->tiv", table, lower, preferred_element_type=jnp.float32)
    return first + second


def slot_products(
    local_blocks, local_rows, local_cols, slot_count, rows_side, cols_side, group_size, group_limit
):
    block_size = local_blocks.shape[1]
    vec_width = rows_side.shape[1]
    row_tiles = rows_side.reshape(-1, block_size, vec_width)
    col_tiles = cols_side.reshape(-1, block_size, vec_width)
    row_count = row_tiles.shape[0]
    col_count = col_tiles.shape[0]

    def group_step(position, totals):
        row_totals, col_totals = totals
        first_slot = position * group_size
        block_tile = lax.dynamic_slice_in_dim(local_blocks, first_slot, group_size, 0)
        rows_here = lax.dynamic_slice_in_dim(local_rows, first_slot, group_size, 0)
        cols_here = lax.dynamic_slice_in_dim(local_cols, first_slot, group_size, 0)
        live_mask = (first_slot + jnp.arange(group_size) < slot_count).astype(jnp.float32)[
            :, None, None
        ]
        row_table = pick_table(rows_here, row_count)
        col_table = pick_table(cols_here, col_count)
        col_picked = jnp.einsum(
            "gt,tjv->gjv", col_table, col_tiles, preferred_element_type=jnp.float32
        ).astype(jnp.bfloat16)
        row_picked = jnp.einsum(
            "gt,tjv->gjv", row_table, row_tiles, preferred_element_type=jnp.float32
        ).astype(jnp.bfloat16)
        forward = (
            jnp.einsum("gij,gjv->giv", block_tile, col_picked, preferred_element_type=jnp.float32)
            * live_mask
        )
        mirror = (
            jnp.einsum("gji,gjv->giv", block_tile, row_picked, preferred_element_type=jnp.float32)
            * live_mask
        )
        return (
            row_totals + place_sum(row_table, forward),
            col_totals + place_sum(col_table, mirror),
        )

    start_totals = (
        jnp.zeros(row_tiles.shape, jnp.float32),
        jnp.zeros(col_tiles.shape, jnp.float32),
    )
    row_totals, col_totals = lax.fori_loop(0, group_limit, group_step, start_totals)
    return (row_totals.reshape(-1, vec_width), col_totals.reshape(-1, vec_width))


def per_device(vectors, blocks, block_rows, block_cols, block_count, lower_edge, upper_edge):
    center = (upper_edge[0] + lower_edge[0]) * 0.5
    half_width = (upper_edge[0] - lower_edge[0]) * 0.5
    local_blocks = blocks[0, 0]
    local_rows = block_rows[0, 0]
    local_cols = block_cols[0, 0]
    slot_count = block_count[0, 0]
    group_size = min(64, local_blocks.shape[0])
    group_limit = local_blocks.shape[0] // group_size
    current = vectors.astype(jnp.float32)
    previous = jnp.zeros_like(current)
    for degree in range(DEGREE):
        operand = current.astype(jnp.bfloat16)
        cols_side = lax.all_gather(operand, "row", axis=0, tiled=True)
        rows_side = lax.all_gather(operand, "col", axis=0, tiled=True)
        row_part, col_part = slot_products(
            local_blocks,
            local_rows,
            local_cols,
            slot_count,
            rows_side,
            cols_side,
            group_size,
            group_limit,
        )
        forward = lax.psum_scatter(row_part, "col", scatter_dimension=0, tiled=True)
        applied = forward + lax.psum_scatter(col_part, "row", scatter_dimension=0, tiled=True)
        shifted = applied - center * current
        if degree == 0:
            following = shifted / half_width
        else:
            following = 2.0 * shifted / half_width - previous
        previous, current = (current, following)
    return current


def link_kernel(
    col_blocks, rows_ref, cols_ref, count_ref, blocks_hbm, table_ref, sums_ref, held, follow, repeats, sem
):
    slots = blocks_hbm.shape[2]
    empty = follow.shape[0] - 1
    count = count_ref[0, 0]
    load = pltpu.make_async_copy(blocks_hbm.at[0, 0], held, sem)
    load.start()

    def clear(i, carry):
        for k in range(16):
            table_ref[i * 16 + k] = empty
        return carry

    lax.fori_loop(0, table_ref.shape[0] // 16, clear, 0)
    follow[empty] = -1

    def link(slot, found):
        place = rows_ref[0, 0, slot] * col_blocks + cols_ref[0, 0, slot]
        before = table_ref[place]
        follow[slot] = before
        table_ref[place] = slot
        repeats[found] = place
        return found + jnp.where(follow[before] == empty, 1, 0)

    found = lax.fori_loop(0, count, link, 0)
    load.wait()

    def sum_place(i, carry):
        place = repeats[i]
        last = table_ref[place]

        def more(state):
            return state[0] != empty

        def add(state):
            at, total = state
            return follow[at], total + held[at].astype(jnp.float32)

        _, total = lax.while_loop(more, add, (follow[last], held[last].astype(jnp.float32)))
        sums_ref[i] = total.astype(sums_ref.dtype)
        table_ref[place] = slots + i
        return carry

    lax.fori_loop(0, found, sum_place, 0)


def link_call(blocks, block_rows, block_cols, block_count, row_blocks, col_blocks):
    _, _, slots, block, _ = blocks.shape
    sums = slots // 2
    smem = pl.BlockSpec(memory_space=pltpu.SMEM)
    return pl.pallas_call(
        functools.partial(link_kernel, col_blocks),
        out_shape=(
            jax.ShapeDtypeStruct((row_blocks * col_blocks,), jnp.int32),
            jax.ShapeDtypeStruct((sums, block, block), jnp.bfloat16),
        ),
        in_specs=[smem] * 3 + [pl.BlockSpec(memory_space=pl.ANY)],
        out_specs=(smem, pl.BlockSpec(memory_space=pltpu.VMEM)),
        scratch_shapes=[
            pltpu.VMEM((slots, block, block), jnp.bfloat16),
            pltpu.SMEM((slots + sums + 1,), jnp.int32),
            pltpu.SMEM((slots + 1,), jnp.int32),
            pltpu.SemaphoreType.DMA,
        ],
        compiler_params=pltpu.CompilerParams(vmem_limit_bytes=62 * 2**20),
        name="link",
    )(block_rows, block_cols, block_count, blocks)


GATHER = (
    (0, None, 1), (0, 0, 2), (0, 1, 4), (0, 1, 2), (0, 0, 4),
    (2, 0, 4), (4, 1, 2),
    (2, None, 1), (4, None, 1),
    (6, 0, 1), (6, 1, 1),
)


def filter_kernel(
    n_row, n_col, x_ref, lower_ref, upper_ref, table_ref, blocks_hbm, sums_hbm, out_ref,
    pool, dense, rows, cols, mirror_t, forward, current, previous,
    core_out, core_in, diag_out, diag_in, quad_out, quad_in,
    up_out, up_in, down_out, down_in,
    pool_sem, gather_send, gather_recv, chain_up_send, chain_down_send, chain_recv,
    core_send, core_recv, diag_send, diag_recv, quad_send, quad_recv,
    up_send, up_recv, down_send, down_recv,
):
    seg = x_ref.shape[0]
    half = seg // 2
    halves = (pl.ds(0, half), pl.ds(half, half))
    f32, bf16 = jnp.float32, jnp.bfloat16
    r = lax.axis_index("row")
    c = lax.axis_index("col")
    core, along_x, along_y = c % 2, (c // 2) % 2, c // 4
    has_up, has_down = r < n_row - 1, r > 0

    def peer(j):
        y = 1 - along_y if j & 4 else along_y
        x = 1 - along_x if j & 2 else along_x
        k = 1 - core if j & 1 else core
        return y * 4 + x * 2 + k

    def send(src, dst, send_sem, recv_sem, device):
        return pltpu.make_async_remote_copy(
            src_ref=src, dst_ref=dst, send_sem=send_sem, recv_sem=recv_sem,
            device_id=device, device_id_type=MESH,
        )

    slots, sums = blocks_hbm.shape[2], sums_hbm.shape[0]
    loads = (
        pltpu.make_async_copy(blocks_hbm.at[0, 0], pool.at[pl.ds(0, slots)], pool_sem.at[0]),
        pltpu.make_async_copy(sums_hbm, pool.at[pl.ds(slots, sums)], pool_sem.at[1]),
    )
    for load in loads:
        load.start()
    pool[slots + sums] = jnp.zeros(pool.shape[1:], pool.dtype)

    barrier = pltpu.get_barrier_semaphore()
    for j in (1, 2, 4):
        pl.semaphore_signal(barrier, inc=1, device_id=(r, peer(j)), device_id_type=MESH)

    @pl.when(has_up)
    def _():
        pl.semaphore_signal(barrier, inc=1, device_id=(r + 1, c), device_id_type=MESH)

    @pl.when(has_down)
    def _():
        pl.semaphore_signal(barrier, inc=1, device_id=(r - 1, c), device_id_type=MESH)

    pl.semaphore_wait(barrier, 3 + jnp.where(has_up, 1, 0) + jnp.where(has_down, 1, 0))

    center = (upper_ref[0] + lower_ref[0]) * 0.5
    half_width = (upper_ref[0] - lower_ref[0]) * 0.5

    def gather(g, i):
        slot, part, to = GATHER[i]
        src, dst = rows.at[g, slot], rows.at[g, slot ^ to]
        if part is not None:
            src, dst = src.at[halves[part]], dst.at[halves[part]]
        return send(src, dst, gather_send.at[g, i], gather_recv.at[g, i], (r, peer(to)))

    def chain_up(g, q, p):
        part = cols.at[g, q, halves[p]]
        return send(part, part, chain_up_send.at[g, q, p], chain_recv.at[g, q, p], (r + 1, c))

    def chain_down(g, q, p):
        part = cols.at[g, q, halves[p]]
        return send(part, part, chain_down_send.at[g, q, p], chain_recv.at[g, q, p], (r - 1, c))

    def sum_up(g, s, p):
        return send(
            up_out.at[g, s, halves[p]], up_in.at[g, s, halves[p]],
            up_send.at[g, s, p], up_recv.at[g, s, p], (r + 1, c),
        )

    def sum_down(g, s, p):
        return send(
            down_out.at[g, s, halves[p]], down_in.at[g, s, halves[p]],
            down_send.at[g, s, p], down_recv.at[g, s, p], (r - 1, c),
        )

    def core_copy(g, j):
        i = j // 2
        return send(core_out.at[g, i], core_in.at[g, i], core_send.at[g, i], core_recv.at[g, i], (r, peer(1)))

    def diag_copy(g, i):
        return send(diag_out.at[g, i], diag_in.at[g, i], diag_send.at[g, i], diag_recv.at[g, i], (r, peer((2, 4)[i])))

    def quad_copy(g, i, part):
        return send(
            quad_out.at[g, i, halves[part]], quad_in.at[g, i, halves[part]],
            quad_send.at[g, i, part], quad_recv.at[g, i, part], (r, peer((2, 4)[i])),
        )

    block = pool.shape[1]
    per_seg = seg // block

    def assemble(a):
        def one(i, carry):
            row, s = i // n_row, i % n_row
            first = ((a * per_seg + row) * n_row + s) * per_seg
            for k in range(per_seg):
                dense[
                    a, s, pl.ds(pl.multiple_of(row * block, block), block), pl.ds(k * block, block)
                ] = pool[table_ref[first + k]]
            return carry

        lax.fori_loop(0, per_seg * n_row, one, 0, unroll=4)

    def mirror_step(g, *slots_here):
        segments = [peer(j) for j in slots_here]
        if g == 0:
            for a in segments:
                assemble(a)
        turned = [rows[g, j].T for j in slots_here]

        def one(s, carry):
            product = sum(
                jnp.dot(t, dense[a, s], preferred_element_type=f32) for t, a in zip(turned, segments)
            )
            if 0 in slots_here:
                mirror_t[s] = product
            else:
                mirror_t[s] += product
            return carry

        lax.fori_loop(0, n_row, one, 0, unroll=n_row)

    def forward_step(g, q, first=False):
        def one(a, carry):
            product = jnp.dot(dense[a, q], cols[g, q], preferred_element_type=f32)
            if first:
                forward[a] = product
            else:
                forward[a] += product
            return carry

        lax.fori_loop(0, n_col, one, 0, unroll=4)

    q_last = jnp.where(2 * r < n_row, n_row - 1, 0)

    def forward_last(g, j):
        a = peer(j)
        forward[a] += jnp.dot(dense[a, q_last], cols[g, q_last], preferred_element_type=f32)

    def mirror_of(s, p):
        return mirror_t[s, :, halves[p]].T

    def mirror_last(g, j):
        a = peer(j)
        if g == 0:
            assemble(a)
        turned = rows[g, j].T
        for i in range(n_row):
            s = jnp.where(2 * r < n_row, n_row - 1 - i, i)
            mirror_t[s] += jnp.dot(turned, dense[a, s], preferred_element_type=f32)
            if i == n_row - 1:
                break

            @pl.when(r == 0)
            def _():
                for p in (0, 1):
                    up_out[g, n_row - 1 - i, halves[p]] = mirror_of(n_row - 1 - i, p).astype(bf16)
                    sum_up(g, n_row - 1 - i, p).start()

            @pl.when(r == n_row - 1)
            def _():
                for p in (0, 1):
                    down_out[g, i, halves[p]] = mirror_of(i, p).astype(bf16)
                    sum_down(g, i, p).start()

    def chain_arrive(g, d, p):
        @pl.when(r >= d)
        def _():
            chain_up(g, r - d, p).wait_recv()

            @pl.when(has_up)
            def _():
                chain_up(g, r - d, p).start()

        @pl.when(r < n_row - d)
        def _():
            chain_down(g, r + d, p).wait_recv()

            @pl.when(has_down)
            def _():
                chain_down(g, r + d, p).start()

    def chain_use(g, d):
        @pl.when((r >= d) & (r - d != q_last))
        def _():
            forward_step(g, r - d)

        @pl.when((r < n_row - d) & (r + d != q_last))
        def _():
            forward_step(g, r + d)

    def sum_hop(g, t, p):
        @pl.when(has_down & has_up & (r <= t))
        def _():
            s = r + n_row - 1 - t
            sum_up(g, s, p).wait_recv()
            up_out[g, s, halves[p]] = (mirror_of(s, p) + up_in[g, s, halves[p]].astype(f32)).astype(bf16)
            sum_up(g, s, p).start()

        @pl.when(has_down & has_up & (n_row - 1 - r <= t))
        def _():
            s = t - (n_row - 1 - r)
            sum_down(g, s, p).wait_recv()
            down_out[g, s, halves[p]] = (mirror_of(s, p) + down_in[g, s, halves[p]].astype(f32)).astype(bf16)
            sum_down(g, s, p).start()

    def begin(g, p):
        @pl.when(has_up)
        def _():
            chain_up(g, r, p).start()

        @pl.when(has_down)
        def _():
            chain_down(g, r, p).start()

        for i in ((1, 4), (3, 2))[p]:
            gather(g, i).start()

    current[...] = x_ref[...].astype(f32)
    rows[0, 0] = x_ref[...]
    cols[0, r] = x_ref[...]
    for p in (0, 1):
        begin(0, p)
    gather(0, 0).start()
    for g in range(DEGREE):
        if g > 0:
            gather(g, 0).wait_recv()
            mirror_step(g, 0, 1)
        for i, onward in ((1, 5), (2, 6)):
            gather(g, i).wait_recv()
            gather(g, onward).start()
        chain_arrive(g, 1, 0)
        if g > 0:
            forward_step(g, r, first=True)
        else:
            for load in loads:
                load.wait()
            gather(g, 0).wait_recv()
            mirror_step(g, 0, 1)
        for i, onward in ((3, 7), (4, 8)):
            gather(g, i).wait_recv()
            gather(g, onward).start()
        chain_arrive(g, 1, 1)
        mirror_step(g, 2, 4)
        for i, onward in ((5, 9), (6, 10)):
            gather(g, i).wait_recv()
            gather(g, onward).start()
        if n_row > 2:
            chain_arrive(g, 2, 0)
        for i in (7, 8):
            gather(g, i).wait_recv()
        mirror_step(g, 3, 5)
        mirror_step(g, 6)
        if n_row > 2:
            chain_arrive(g, 2, 1)
        gather(g, 9).wait_recv()
        gather(g, 10).wait_recv()
        mirror_last(g, 7)
        if g == 0:
            forward_step(g, r, first=True)
        chain_use(g, 1)
        for d in range(2, n_row):
            if d > 2:
                for p in (0, 1):
                    chain_arrive(g, d, p)
            chain_use(g, d)

        for j in (7, 3, 5, 1):
            forward_last(g, j)
            core_out[g, j // 2] = forward[peer(j)].astype(bf16)
            core_copy(g, j).start()
        for j in (6, 2, 4, 0):
            forward_last(g, j)
        if n_row > 2:
            sum_hop(g, 1, 0)

        def paired(j):
            return forward[peer(j)] + core_in[g, j // 2].astype(f32)

        core_copy(g, 7).wait_recv()
        total = paired(6).astype(bf16)
        for i in (0, 1):
            diag_out[g, i] = total[i * half:(i + 1) * half]
            diag_copy(g, i).start()
        for i, j, free in ((0, 2, 0), (1, 4, 1)):
            core_copy(g, j + 1).wait_recv()
            forward[peer(j)] = paired(j)
            quad_out[g, i, halves[free]] = forward[peer(j), halves[free]].astype(bf16)
            quad_copy(g, i, free).start()
        if n_row > 2:
            sum_hop(g, 1, 1)
        for i, j, late, source in ((1, 4, 0, 0), (0, 2, 1, 1)):
            diag_copy(g, source).wait_recv()
            quad_out[g, i, halves[late]] = (
                forward[peer(j), halves[late]] + diag_in[g, source].astype(f32)
            ).astype(bf16)
            quad_copy(g, i, late).start()

        for t in range(2, n_row - 1):
            for p in (0, 1):
                sum_hop(g, t, p)
        core_copy(g, 1).wait_recv()
        for p in (0, 1):
            part = halves[p]
            for i in (0, 1):
                quad_copy(g, i, p).wait_recv()
            forward[c, part] += (
                core_in[g, 0, part].astype(f32) + mirror_of(r, p)
                + (quad_in[g, 0, part].astype(f32) + quad_in[g, 1, part].astype(f32))
            )

            @pl.when(has_down)
            def _():
                sum_up(g, r, p).wait_recv()
                forward[c, part] += up_in[g, r, part].astype(f32)

            @pl.when(has_up)
            def _():
                sum_down(g, r, p).wait_recv()
                forward[c, part] += down_in[g, r, part].astype(f32)

            shifted = forward[c, part] - center * current[part]
            if g == 0:
                following = shifted / half_width
            else:
                following = 2.0 * shifted / half_width - previous[part]
            if g == DEGREE - 1:
                out_ref[part] = following
            else:
                previous[part] = current[part]
                current[part] = following
                rows[g + 1, 0, part] = following.astype(bf16)
                cols[g + 1, r, part] = following.astype(bf16)
                begin(g + 1, p)
        if g < DEGREE - 1:
            gather(g + 1, 0).start()

    for g in range(DEGREE):
        for i in range(len(GATHER)):
            gather(g, i).wait_send()
        for j in (1, 3, 5, 7):
            core_copy(g, j).wait_send()
        for i in (0, 1):
            diag_copy(g, i).wait_send()
            for part in (0, 1):
                quad_copy(g, i, part).wait_send()
        for q in range(n_row):
            @pl.when(has_up & (q <= r))
            def _():
                for p in (0, 1):
                    chain_up(g, q, p).wait_send()

            @pl.when(has_down & (q >= r))
            def _():
                for p in (0, 1):
                    chain_down(g, q, p).wait_send()

            @pl.when(q > r)
            def _():
                for p in (0, 1):
                    sum_up(g, q, p).wait_send()

            @pl.when(q < r)
            def _():
                for p in (0, 1):
                    sum_down(g, q, p).wait_send()


def filter_call(vectors, lower_edge, upper_edge, table, blocks, sums, n_row, n_col):
    seg, width = vectors.shape
    half = seg // 2
    f32, bf16 = jnp.float32, jnp.bfloat16
    vmem, dma = pltpu.VMEM, pltpu.SemaphoreType.DMA
    g = DEGREE
    scratch = [
        vmem((blocks.shape[2] + sums.shape[0] + 1,) + sums.shape[1:], bf16),
        vmem((n_col, n_row, seg, seg), bf16),
        vmem((g, n_col, seg, width), bf16),
        vmem((g, n_row, seg, width), bf16),
        vmem((n_row, width, seg), f32),
        vmem((n_col, seg, width), f32),
        vmem((seg, width), f32),
        vmem((seg, width), f32),
        vmem((g, n_col // 2, seg, width), bf16),
        vmem((g, n_col // 2, seg, width), bf16),
        vmem((g, 2, half, width), bf16),
        vmem((g, 2, half, width), bf16),
        vmem((g, 2, seg, width), bf16),
        vmem((g, 2, seg, width), bf16),
    ]
    scratch += [vmem((g, n_row, seg, width), bf16)] * 4
    scratch += [dma((2,))] + [dma((g, len(GATHER)))] * 2 + [dma((g, n_row, 2))] * 3
    scratch += [dma((g, n_col // 2))] * 2 + [dma((g, 2))] * 2 + [dma((g, 2, 2))] * 2
    scratch += [dma((g, n_row, 2))] * 4
    return pl.pallas_call(
        functools.partial(filter_kernel, n_row, n_col),
        out_shape=jax.ShapeDtypeStruct((seg, width), f32),
        in_specs=[
            pl.BlockSpec(memory_space=pltpu.VMEM),
            pl.BlockSpec(memory_space=pltpu.SMEM),
            pl.BlockSpec(memory_space=pltpu.SMEM),
            pl.BlockSpec(memory_space=pltpu.SMEM),
            pl.BlockSpec(memory_space=pl.ANY),
            pl.BlockSpec(memory_space=pl.ANY),
        ],
        out_specs=pl.BlockSpec(memory_space=pltpu.VMEM),
        scratch_shapes=scratch,
        compiler_params=pltpu.CompilerParams(
            collective_id=0, has_side_effects=True, vmem_limit_bytes=62 * 2**20
        ),
        name="filter",
    )(vectors, lower_edge, upper_edge, table, blocks, sums)


def per_device_dense(
    n_row, n_col, vectors, blocks, block_rows, block_cols, block_count, lower_edge, upper_edge
):
    per_seg = vectors.shape[0] // blocks.shape[-1]
    table, sums = link_call(
        blocks, block_rows, block_cols, block_count, n_col * per_seg, n_row * per_seg
    )
    return filter_call(vectors, lower_edge, upper_edge, table, blocks, sums, n_row, n_col)


def per_device_any(n_row, n_col, vectors, *others):
    dense_bytes = 2 * n_row * n_col * vectors.shape[0] ** 2
    if n_col == 8 and n_row >= 2 and dense_bytes <= 16 * 2**20:
        return per_device_dense(n_row, n_col, vectors, *others)
    return per_device(vectors, *others)


def solution(mesh):
    return jax.shard_map(
        functools.partial(per_device_any, mesh.shape["row"], mesh.shape["col"]),
        mesh=mesh,
        in_specs=(
            P(("row", "col"), None),
            P("row", "col", None, None, None),
            P("row", "col", None),
            P("row", "col", None),
            P("row", "col"),
            P(),
            P(),
        ),
        out_specs=P(("row", "col"), None),
        check_vma=False,
    )
```
